512 devices in a mesh: cuts: 64 (over x, z_lo, core), ang: 8 (over y, z_hi).
Axes of the slice: x: 4, y: 4, z: 16 (z_hi: 2, z_lo: 8; z = z_hi * 8 + z_lo), core: 2. Of those that a mesh axis runs over, the one named last changes fastest.
Arguments:
- projections: bfloat16 [64, 64, 8, 32, 256], P('cuts', None, 'ang'), may hold values from -48 to 48
- start_image: bfloat16 [16384, 1024], P('cuts'), may hold values from 0 to 2
- system: bfloat16 [32, 16, 2, 64, 128], P('ang'), may hold values from 0.0009994507 to 0.029907227
- first_tile: int32 [32, 16], P('ang'), may hold values from 0 to 3, as said below
Outputs:
- new_image: float32 [16384, 1024], P('cuts', 'ang')
- residual: bfloat16 [64, 16384, 256], P('ang', 'cuts')
The draws below stay inside these ranges and needn't reach their ends.
Inputs may be any that keep to these rules, and one draw needn't show every extreme that they name: In every angle block each bin tile is first_tile of at least one pixel tile; every pixel tile meets exactly two bin tiles, first_tile and first_tile + 1 modulo 4.
All inputs are finite; a program needn't handle non-finite values.
Results may differ from the reference program's by a relative error of at most 0.001.
Values may be sent and summed in bfloat16 or wider, within the bound.
No kernel may reach another device: no remote copies, remote signals or barrier semaphores. Data moves between devices by JAX's collectives and lax.ppermute only.
A program may use at most 128 MiB of HBM per device.

```python
import jax
import jax.numpy as jnp
from jax import lax

TILE_WIDTH = 64
PAIR_ANG = 2
BIN_TILE_COUNT = 4
PIXEL_TILES = 16
ANGLE_COUNT = 64
BLOCKS = 32
ROWS = 16384
SLICE_BLOCKS = 64
ROW_GROUPS = 8
GROUP_SLICES = 32
NPIX = 1024
DETECTOR_BINS = 256


def draw_first_tile(key, part):
    base_key = jax.random.fold_in(key, 31)
    order_key = jax.random.fold_in(key, 47)
    base = jax.random.randint(base_key, (BLOCKS, PIXEL_TILES), 0, BIN_TILE_COUNT, dtype=jnp.int32)

    def one_order(subkey):
        return jax.random.permutation(subkey, PIXEL_TILES)
    orders = jax.vmap(one_order)(jax.random.split(order_key, BLOCKS))
    ranks = jnp.argsort(orders, axis=1, stable=True).astype(jnp.int32)
    return jnp.where(ranks < BIN_TILE_COUNT, ranks, base).astype(jnp.int32)


def levels(rng, shape, cuts, least, high):
    def one(dim, shards_of):
        draws = jax.random.uniform(jax.random.fold_in(jax.random.fold_in(rng, 6), dim), (shards_of,), jnp.float32, least / len(cuts), high / len(cuts))
        return jnp.repeat(jnp.exp(draws), shape[dim] // shards_of).reshape((-1,) + (1,) * (len(shape) - dim - 1))

    factor_of = one(*cuts[0])
    for cut in cuts[1:]:
        factor_of = factor_of * one(*cut)
    return factor_of


def scatter_about(stream_key, shape, spread, bound, cuts=(), kind=jnp.bfloat16):
    level = levels(stream_key, shape, cuts, -0.22, 0.18) if cuts else 1.0
    result = jax.random.normal(stream_key, shape, jnp.float32) * spread * level
    return jnp.minimum(jnp.maximum(result, -bound), bound).astype(kind)


def setup_inputs(seed: int = 0) -> dict:
    key_of = jax.random.split(jax.random.key(seed), 5)
    return {
        "projections": scatter_about(key_of[0], (ANGLE_COUNT, SLICE_BLOCKS, ROW_GROUPS, GROUP_SLICES, DETECTOR_BINS), (0.031 * TILE_WIDTH * PIXEL_TILES / BIN_TILE_COUNT), 48.0, ((0, 64), (2, 8))),
        "start_image": jnp.clip(2.0 * jax.random.uniform(key_of[1], (ROWS, NPIX), jnp.float32) ** levels(key_of[1], (ROWS, NPIX), ((0, 64),), -0.2, 0.2), 0.0, 2.0).astype(jnp.bfloat16),
        "system": jnp.clip(0.0009994507 + 0.028907776 * jax.random.uniform(key_of[2], (BLOCKS, PIXEL_TILES, 2, TILE_WIDTH, PAIR_ANG * TILE_WIDTH), jnp.float32) ** levels(key_of[2], (BLOCKS, PIXEL_TILES, 2, TILE_WIDTH, PAIR_ANG * TILE_WIDTH), ((0, 8),), -0.2, 0.2), 0.0009994507, 0.029907227).astype(jnp.bfloat16),
        "first_tile": draw_first_tile(jax.random.fold_in(key_of[4], 71), 0),
    }


def reference(projections, start_image, system, first_tile):
    sinogram = projections.reshape(BLOCKS, PAIR_ANG, ROWS, DETECTOR_BINS)
    pixels = start_image.astype(jnp.float32).reshape(ROWS, PIXEL_TILES, TILE_WIDTH)
    tile_ids = jnp.arange(BIN_TILE_COUNT, dtype=jnp.int32)
    highest = lax.Precision.HIGHEST

    def step_block(carry, inputs):
        backproj, col_total = carry
        weights, first, measured = inputs
        weights = weights.astype(jnp.float32)
        bin_index = jnp.stack([first, (first + 1) % BIN_TILE_COUNT], axis=1)
        onehot = (bin_index[:, :, None] == tile_ids).astype(jnp.float32)
        partial_value = jnp.einsum('rpi,pjic->pjrc', pixels, weights, precision=highest)
        forward = jnp.einsum('pjb,pjrc->brc', onehot, partial_value, precision=highest)
        row_total = jnp.einsum('pjb,pjc->bc', onehot, jnp.sum(weights, axis=2), precision=highest)
        measured_t = measured.astype(jnp.float32).reshape(PAIR_ANG, ROWS, BIN_TILE_COUNT, TILE_WIDTH)
        measured_t = measured_t.transpose(2, 1, 0, 3).reshape(BIN_TILE_COUNT, ROWS, PAIR_ANG * TILE_WIDTH)
        resid = ((measured_t - forward) / row_total[:, None, :]).astype(jnp.bfloat16)
        resid = lax.optimization_barrier(resid)
        picked = jnp.einsum('pjb,brc->pjrc', onehot, resid.astype(jnp.float32), precision=highest)
        backproj = backproj + jnp.einsum('pjrc,pjic->rpi', picked, weights, precision=highest)
        col_total = col_total + jnp.sum(weights, axis=(1, 3))
        out_block = resid.reshape(BIN_TILE_COUNT, ROWS, PAIR_ANG, TILE_WIDTH).transpose(2, 1, 0, 3).reshape(PAIR_ANG, ROWS, DETECTOR_BINS)
        return (backproj, col_total), out_block

    start = (jnp.zeros((ROWS, PIXEL_TILES, TILE_WIDTH), jnp.float32), jnp.zeros((PIXEL_TILES, TILE_WIDTH), jnp.float32))
    (backproj, col_total), blocks_out = lax.scan(step_block, start, (system, first_tile, sinogram))
    residual = blocks_out.reshape(ANGLE_COUNT, ROWS, DETECTOR_BINS)
    new_image = start_image.astype(jnp.float32) + (backproj / col_total[None, :, :]).reshape(ROWS, NPIX)
    return new_image, residual
```

```python
import functools

import jax
import jax.numpy as jnp
from jax import lax
from jax.experimental import pallas as pl
from jax.experimental.pallas import tpu as pltpu
from jax.sharding import Mesh
from jax.sharding import PartitionSpec as P

AXES = ("x", "zl", "core", "y", "zh")
SIZES = (4, 8, 2, 4, 2)
F32 = jnp.float32
BF16 = jnp.bfloat16


def index_of(x, zl, core, y, zh):
    return (((x * 8 + zl) * 2 + core) * 4 + y) * 2 + zh


def pairs(dest):
    out = []
    for x in range(4):
        for zl in range(8):
            for core in range(2):
                for y in range(4):
                    for zh in range(2):
                        out.append((index_of(x, zl, core, y, zh), index_of(*dest(x, zl, core, y, zh))))
    return out


def contract(a, b, da, db):
    return lax.dot_general(a, b, (((da,), (db,)), ((), ())), preferred_element_type=F32)


def prepare_kernel(first_ref, image_ref, system_ref, a_ref, fwd_ref, rinv_ref, col_ref):
    g = pl.program_id(0)
    low = lax.broadcasted_iota(jnp.int32, (64, 128), 1) < 64
    for p in range(16):
        f = first_ref[g, p]
        t0 = system_ref[0, p, 0].astype(F32)
        t1 = system_ref[0, p, 1].astype(F32)
        even = f % 2 == 0
        e = jnp.where(even, t0, t1)
        o = jnp.where(even, t1, t0)
        x0 = jnp.where(low, e, pltpu.roll(o, 64, 1))
        x1 = jnp.where(low, pltpu.roll(e, 64, 1), o)
        ve = jnp.where((f == 1) | (f == 2), 1, 0)
        vo = jnp.where(f >= 2, 1, 0)
        place = jnp.where(low, ve, vo)
        for t, xt in ((0, x0), (1, x1)):
            for v in range(2):
                a_ref[0, p * 64 : (p + 1) * 64, t * 256 + v * 128 : t * 256 + (v + 1) * 128] = jnp.where(
                    place == v, xt, 0.0
                ).astype(BF16)
    a = a_ref[0]
    fwd_ref[0] = contract(image_ref[...], a, 1, 0)
    rows = contract(jnp.ones((8, 1024), BF16), a, 1, 0)
    rinv_ref[0] = 1.0 / rows
    cols = contract(jnp.ones((8, 512), BF16), a, 1, 1)

    @pl.when(g == 0)
    def _():
        col_ref[...] = cols

    @pl.when(g > 0)
    def _():
        col_ref[...] += cols


def prepare(first, image, system):
    return pl.pallas_call(
        prepare_kernel,
        grid=(4,),
        in_specs=[
            pl.BlockSpec(memory_space=pltpu.SMEM),
            pl.BlockSpec((256, 1024), lambda g: (0, 0)),
            pl.BlockSpec((1, 16, 2, 64, 128), lambda g: (g, 0, 0, 0, 0)),
        ],
        out_specs=[
            pl.BlockSpec((1, 1024, 512), lambda g: (g, 0, 0)),
            pl.BlockSpec((1, 256, 512), lambda g: (g, 0, 0)),
            pl.BlockSpec((1, 8, 512), lambda g: (g, 0, 0)),
            pl.BlockSpec((8, 1024), lambda g: (0, 0)),
        ],
        out_shape=[
            jax.ShapeDtypeStruct((4, 1024, 512), BF16),
            jax.ShapeDtypeStruct((4, 256, 512), F32),
            jax.ShapeDtypeStruct((4, 8, 512), F32),
            jax.ShapeDtypeStruct((8, 1024), F32),
        ],
        cost_estimate=pl.CostEstimate(flops=1100000000, bytes_accessed=10000000, transcendentals=0),
        compiler_params=pltpu.CompilerParams(vmem_limit_bytes=40 * 1024 * 1024),
        name="prepare",
    )(first, image, system)


def finish_kernel(where_ref, *refs):
    chunks, (a_ref, fwd_ref, rinv_ref, col_ref, res_ref, part_ref, held_ref) = refs[:8], refs[8:]
    dh, dl = where_ref[0], where_ref[1]
    for b in range(4):
        g = dl ^ b
        for a in range(2):
            zh = dh ^ a
            chunk = chunks[a * 4 + b]
            for t in range(2):
                rinv = rinv_ref[g, 0:1, t * 256 : (t + 1) * 256]
                for y in range(4):
                    rows = pl.ds(pl.multiple_of((y * 2 + zh) * 32, 32), 32)
                    lanes = slice(t * 256, (t + 1) * 256)
                    res = ((chunk[t * 4 + y].astype(F32) - fwd_ref[g, rows, lanes]) * rinv).astype(BF16)
                    res_ref[g * 2 + t, rows, :] = res
                    held_ref[rows, lanes] = res
        for q in range(4):
            add = contract(held_ref[...], a_ref[g, q * 256 : (q + 1) * 256, :], 1, 1)
            if b == 0:
                part_ref[q, 0:256, :] = add
            else:
                part_ref[q, 0:256, :] += add
    for q in range(4):
        part_ref[q, 256:264, :] = col_ref[:, q * 256 : (q + 1) * 256]


def finish(where, chunks, a, fwd, rinv, col):
    vmem = pl.BlockSpec(memory_space=pltpu.VMEM)
    return pl.pallas_call(
        finish_kernel,
        in_specs=[pl.BlockSpec(memory_space=pltpu.SMEM)] + [vmem] * 12,
        out_specs=[vmem, vmem],
        out_shape=[
            jax.ShapeDtypeStruct((8, 256, 256), BF16),
            jax.ShapeDtypeStruct((4, 264, 256), F32),
        ],
        scratch_shapes=[pltpu.VMEM((256, 512), BF16)],
        cost_estimate=pl.CostEstimate(flops=1100000000, bytes_accessed=10000000, transcendentals=0),
        compiler_params=pltpu.CompilerParams(vmem_limit_bytes=40 * 1024 * 1024),
        name="finish",
    )(where, *chunks, a, fwd, rinv, col)


def on_device(projections, start_image, system, first_tile):
    zl, y, zh = lax.axis_index("zl"), lax.axis_index("y"), lax.axis_index("zh")
    dh, dl = zl // 4, zl % 4
    sent = projections.reshape(4, 8, 2, 32, 256).transpose(2, 0, 1, 3, 4).reshape(8, 8, 32, 256)
    sent = lax.all_to_all(sent, ("core", "y"), 0, 0, tiled=True)
    chunks = []
    for k in range(8):

        def dest(x, zl, core, y, zh, k=k):
            return (y, (zh * 4 + zl % 4) ^ k, core, x, zl // 4)

        block = lax.dynamic_index_in_dim(sent, (zh * 4 + dl) ^ k, 1, keepdims=False)
        chunks.append(lax.ppermute(block, AXES, pairs(dest)))
    first_tile, image, system, _ = lax.optimization_barrier((first_tile, start_image, system, sent))
    a, fwd, rinv, col = prepare(first_tile, image, system)
    where = jnp.stack([dh, dl]).astype(jnp.int32)
    residual, part = finish(where, chunks, a, fwd, rinv, col)
    part = lax.all_to_all(part, "y", 0, 0, tiled=True).sum(0)
    halves = jnp.stack([part[:, :128], part[:, 128:]])
    mine = lax.dynamic_index_in_dim(halves, zh, 0, keepdims=False)
    other = lax.dynamic_index_in_dim(halves, 1 - zh, 0, keepdims=False)
    swap = pairs(lambda x, zl, core, y, zh: (x, zl, core, y, 1 - zh))
    total = mine + lax.ppermute(other, AXES, swap)
    local = lax.dynamic_slice_in_dim(start_image, (y * 2 + zh) * 128, 128, 1).astype(F32)
    new_image = local + total[:256] / total[256:257]
    return new_image, residual


def solution(mesh):
    mesh = Mesh(mesh.devices.reshape(SIZES), AXES)
    cuts, ang = ("x", "zl", "core"), ("y", "zh")
    in_specs = (
        P(cuts, None, ang, None, None),
        P(cuts, None),
        P(ang, None, None, None, None),
        P(ang, None),
    )
    out_specs = (P(cuts, ang), P(ang, cuts, None))
    return jax.shard_map(on_device, mesh=mesh, in_specs=in_specs, out_specs=out_specs, check_vma=False)
```

```python
import functools

import jax
import jax.numpy as jnp
from jax import lax
from jax.experimental import pallas as pl
from jax.experimental.pallas import tpu as pltpu
from jax.sharding import Mesh
from jax.sharding import PartitionSpec as P

AXES = ("x", "zl", "core", "y", "zh")
SIZES = (4, 8, 2, 4, 2)
F32 = jnp.float32
BF16 = jnp.bfloat16


def index_of(x, zl, core, y, zh):
    return (((x * 8 + zl) * 2 + core) * 4 + y) * 2 + zh


def pairs(dest):
    out = []
    for x in range(4):
        for zl in range(8):
            for core in range(2):
                for y in range(4):
                    for zh in range(2):
                        out.append((index_of(x, zl, core, y, zh), index_of(*dest(x, zl, core, y, zh))))
    return out


def contract(a, b, da, db):
    return lax.dot_general(a, b, (((da,), (db,)), ((), ())), preferred_element_type=F32)


def prepare_kernel(first_ref, image_ref, system_ref, a_ref, fwd_ref, rinv_ref, col_ref):
    g = pl.program_id(0)
    low = lax.broadcasted_iota(jnp.int32, (64, 128), 1) < 64
    for p in range(16):
        f = first_ref[g, p]
        t0 = system_ref[0, p, 0].astype(F32)
        t1 = system_ref[0, p, 1].astype(F32)
        even = f % 2 == 0
        e = jnp.where(even, t0, t1)
        o = jnp.where(even, t1, t0)
        x0 = jnp.where(low, e, pltpu.roll(o, 64, 1))
        x1 = jnp.where(low, pltpu.roll(e, 64, 1), o)
        ve = jnp.where((f == 1) | (f == 2), 1, 0)
        vo = jnp.where(f >= 2, 1, 0)
        place = jnp.where(low, ve, vo)
        for t, xt in ((0, x0), (1, x1)):
            for v in range(2):
                a_ref[0, p * 64 : (p + 1) * 64, t * 256 + v * 128 : t * 256 + (v + 1) * 128] = jnp.where(
                    place == v, xt, 0.0
                ).astype(BF16)
    a = a_ref[0]
    fwd_ref[0] = contract(image_ref[...], a, 1, 0)
    rows = contract(jnp.ones((8, 1024), BF16), a, 1, 0)
    rinv_ref[0] = 1.0 / rows
    cols = contract(jnp.ones((8, 512), BF16), a, 1, 1)

    @pl.when(g == 0)
    def _():
        col_ref[...] = cols

    @pl.when(g > 0)
    def _():
        col_ref[...] += cols


def prepare(first, image, system):
    return pl.pallas_call(
        prepare_kernel,
        grid=(4,),
        in_specs=[
            pl.BlockSpec(memory_space=pltpu.SMEM),
            pl.BlockSpec((256, 1024), lambda g: (0, 0)),
            pl.BlockSpec((1, 16, 2, 64, 128), lambda g: (g, 0, 0, 0, 0)),
        ],
        out_specs=[
            pl.BlockSpec((1, 1024, 512), lambda g: (g, 0, 0)),
            pl.BlockSpec((1, 256, 512), lambda g: (g, 0, 0)),
            pl.BlockSpec((1, 8, 512), lambda g: (g, 0, 0)),
            pl.BlockSpec((8, 1024), lambda g: (0, 0)),
        ],
        out_shape=[
            jax.ShapeDtypeStruct((4, 1024, 512), BF16),
            jax.ShapeDtypeStruct((4, 256, 512), F32),
            jax.ShapeDtypeStruct((4, 8, 512), F32),
            jax.ShapeDtypeStruct((8, 1024), F32),
        ],
        cost_estimate=pl.CostEstimate(flops=1100000000, bytes_accessed=10000000, transcendentals=0),
        compiler_params=pltpu.CompilerParams(vmem_limit_bytes=40 * 1024 * 1024),
        name="prepare",
    )(first, image, system)


def finish_kernel(where_ref, *refs):
    near_ref, far_refs, (a_ref, fwd_ref, rinv_ref, col_ref, res_ref, part_ref, held_ref) = refs[0], refs[1:5], refs[5:]
    dh, dl, own_y = where_ref[0], where_ref[1], where_ref[2]
    for b in range(4):
        g = dl ^ b
        for a in range(2):
            zh = dh ^ a
            for t in range(2):
                rinv = rinv_ref[g, 0:1, t * 256 : (t + 1) * 256]
                for y in range(4):
                    rows = pl.ds(pl.multiple_of((y * 2 + zh) * 32, 32), 32)
                    lanes = slice(t * 256, (t + 1) * 256)
                    block = near_ref[(y ^ own_y) * 2 + t, b] if a == 0 else far_refs[b][t * 4 + y]
                    res = ((block.astype(F32) - fwd_ref[g, rows, lanes]) * rinv).astype(BF16)
                    res_ref[g * 2 + t, rows, :] = res
                    held_ref[rows, lanes] = res
        for q in range(4):
            add = contract(held_ref[...], a_ref[g, q * 256 : (q + 1) * 256, :], 1, 1)
            if b == 0:
                part_ref[q, 0:256, :] = add
            else:
                part_ref[q, 0:256, :] += add
    for q in range(4):
        part_ref[q, 256:264, :] = col_ref[:, q * 256 : (q + 1) * 256]


def finish(where, near, far, a, fwd, rinv, col):
    vmem = pl.BlockSpec(memory_space=pltpu.VMEM)
    return pl.pallas_call(
        finish_kernel,
        in_specs=[pl.BlockSpec(memory_space=pltpu.SMEM)] + [vmem] * 9,
        out_specs=[vmem, vmem],
        out_shape=[
            jax.ShapeDtypeStruct((8, 256, 256), BF16),
            jax.ShapeDtypeStruct((4, 264, 256), F32),
        ],
        scratch_shapes=[pltpu.VMEM((256, 512), BF16)],
        cost_estimate=pl.CostEstimate(flops=1100000000, bytes_accessed=10000000, transcendentals=0),
        compiler_params=pltpu.CompilerParams(vmem_limit_bytes=40 * 1024 * 1024),
        name="finish",
    )(where, near, *far, a, fwd, rinv, col)


def on_device(projections, start_image, system, first_tile):
    x, zl, y, zh = (lax.axis_index(name) for name in ("x", "zl", "y", "zh"))
    dh, dl = zl // 4, zl % 4
    mine = zh * 4 + dl
    blocks = projections.reshape(4, 2, 4, 2, 32, 256)

    def send(block, k):
        def dest(x, zl, core, y, zh):
            return (x ^ y, (zh * 4 + zl % 4) ^ k, core, x, zl // 4)

        return lax.ppermute(block, AXES, pairs(dest))

    near = lax.dynamic_index_in_dim(blocks, zh, 1, keepdims=False)
    near = [lax.dynamic_index_in_dim(near, dl ^ b, 1, keepdims=False) for b in range(4)]
    first_tile, image, system, near = lax.optimization_barrier((first_tile, start_image, system, near))
    far = lax.dynamic_index_in_dim(blocks, 1 - zh, 1, keepdims=False)
    far = jnp.stack([lax.dynamic_index_in_dim(far, x ^ m, 0, keepdims=False) for m in range(4)])
    far = far.transpose(2, 0, 1, 3, 4).reshape(8, 4, 32, 256)
    near = [send(block.reshape(8, 32, 256), b) for b, block in enumerate(near)]
    far = lax.all_to_all(far, ("core", "y"), 0, 0, tiled=True)
    near, _ = lax.optimization_barrier((near, far))
    far = [lax.dynamic_index_in_dim(far, dl ^ b, 1, keepdims=False) for b in range(4)]
    near = jnp.stack(near, 1)
    far = [send(block, 4 + b) for b, block in enumerate(far)]
    near = lax.all_to_all(near, ("x", "core"), 0, 0, tiled=True)
    a, fwd, rinv, col = prepare(first_tile, image, system)
    where = jnp.stack([dh, dl, y]).astype(jnp.int32)
    residual, part = finish(where, near, far, a, fwd, rinv, col)
    part = lax.all_to_all(part, "y", 0, 0, tiled=True).sum(0)
    halves = jnp.stack([part[:, :128], part[:, 128:]])
    mine = lax.dynamic_index_in_dim(halves, zh, 0, keepdims=False)
    other = lax.dynamic_index_in_dim(halves, 1 - zh, 0, keepdims=False)
    swap = pairs(lambda x, zl, core, y, zh: (x, zl, core, y, 1 - zh))
    total = mine + lax.ppermute(other, AXES, swap)
    local = lax.dynamic_slice_in_dim(start_image, (y * 2 + zh) * 128, 128, 1).astype(F32)
    new_image = local + total[:256] / total[256:257]
    return new_image, residual


def solution(mesh):
    mesh = Mesh(mesh.devices.reshape(SIZES), AXES)
    cuts, ang = ("x", "zl", "core"), ("y", "zh")
    in_specs = (
        P(cuts, None, ang, None, None),
        P(cuts, None),
        P(ang, None, None, None, None),
        P(ang, None),
    )
    out_specs = (P(cuts, ang), P(ang, cuts, None))
    return jax.shard_map(on_device, mesh=mesh, in_specs=in_specs, out_specs=out_specs, check_vma=False)
```

```python
import functools

import jax
import jax.numpy as jnp
from jax import lax
from jax.experimental import pallas as pl
from jax.experimental.pallas import tpu as pltpu
from jax.sharding import Mesh
from jax.sharding import PartitionSpec as P

AXES = ("x", "zl", "core", "y", "zh")
SIZES = (4, 8, 2, 4, 2)
F32 = jnp.float32
BF16 = jnp.bfloat16


def index_of(x, zl, core, y, zh):
    return (((x * 8 + zl) * 2 + core) * 4 + y) * 2 + zh


def pairs(dest):
    out = []
    for x in range(4):
        for zl in range(8):
            for core in range(2):
                for y in range(4):
                    for zh in range(2):
                        out.append((index_of(x, zl, core, y, zh), index_of(*dest(x, zl, core, y, zh))))
    return out


def contract(a, b, da, db):
    return lax.dot_general(a, b, (((da,), (db,)), ((), ())), preferred_element_type=F32)


def prepare_kernel(first_ref, image_ref, system_ref, a_ref, fwd_ref, rinv_ref, col_ref):
    g = pl.program_id(0)
    low = lax.broadcasted_iota(jnp.int32, (64, 128), 1) < 64
    for p in range(16):
        f = first_ref[g, p]
        t0 = system_ref[0, p, 0].astype(F32)
        t1 = system_ref[0, p, 1].astype(F32)
        even = f % 2 == 0
        e = jnp.where(even, t0, t1)
        o = jnp.where(even, t1, t0)
        x0 = jnp.where(low, e, pltpu.roll(o, 64, 1))
        x1 = jnp.where(low, pltpu.roll(e, 64, 1), o)
        ve = jnp.where((f == 1) | (f == 2), 1, 0)
        vo = jnp.where(f >= 2, 1, 0)
        place = jnp.where(low, ve, vo)
        for t, xt in ((0, x0), (1, x1)):
            for v in range(2):
                a_ref[0, p * 64 : (p + 1) * 64, t * 256 + v * 128 : t * 256 + (v + 1) * 128] = jnp.where(
                    place == v, xt, 0.0
                ).astype(BF16)
    a = a_ref[0]
    fwd_ref[0] = contract(image_ref[...], a, 1, 0)
    rows = contract(jnp.ones((8, 1024), BF16), a, 1, 0)
    rinv_ref[0] = 1.0 / rows
    cols = contract(jnp.ones((8, 512), BF16), a, 1, 1)

    @pl.when(g == 0)
    def _():
        col_ref[...] = cols

    @pl.when(g > 0)
    def _():
        col_ref[...] += cols


def prepare(first, image, system):
    return pl.pallas_call(
        prepare_kernel,
        grid=(4,),
        in_specs=[
            pl.BlockSpec(memory_space=pltpu.SMEM),
            pl.BlockSpec((256, 1024), lambda g: (0, 0)),
            pl.BlockSpec((1, 16, 2, 64, 128), lambda g: (g, 0, 0, 0, 0)),
        ],
        out_specs=[
            pl.BlockSpec((1, 1024, 512), lambda g: (g, 0, 0)),
            pl.BlockSpec((1, 256, 512), lambda g: (g, 0, 0)),
            pl.BlockSpec((1, 8, 512), lambda g: (g, 0, 0)),
            pl.BlockSpec((8, 1024), lambda g: (0, 0)),
        ],
        out_shape=[
            jax.ShapeDtypeStruct((4, 1024, 512), BF16),
            jax.ShapeDtypeStruct((4, 256, 512), F32),
            jax.ShapeDtypeStruct((4, 8, 512), F32),
            jax.ShapeDtypeStruct((8, 1024), F32),
        ],
        cost_estimate=pl.CostEstimate(flops=1100000000, bytes_accessed=10000000, transcendentals=0),
        compiler_params=pltpu.CompilerParams(vmem_limit_bytes=40 * 1024 * 1024),
        name="prepare",
    )(first, image, system)


def pack_kernel(where_ref, p_ref, n0_ref, n1_ref, n2_ref, n3_ref, far_ref, sems):
    x, dl, zh = where_ref[0], where_ref[1], where_ref[2]
    copies = []
    for b, near_ref in enumerate((n0_ref, n1_ref, n2_ref, n3_ref)):
        low = dl ^ b
        copies.append(pltpu.make_async_copy(p_ref.at[:, (zh ^ (low & 1)) * 4 + low], near_ref, sems.at[b]))
    for m in range(4):
        for low in range(4):
            src = p_ref.at[x ^ m, (zh ^ (low & 1) ^ 1) * 4 + low]
            copies.append(pltpu.make_async_copy(src, far_ref.at[:, m, low], sems.at[4 + m * 4 + low]))
    for copy in copies:
        copy.start()
    for copy in copies:
        copy.wait()


def pack(where, projections):
    vmem = pl.BlockSpec(memory_space=pltpu.VMEM)
    return pl.pallas_call(
        pack_kernel,
        in_specs=[pl.BlockSpec(memory_space=pltpu.SMEM), pl.BlockSpec(memory_space=pl.ANY)],
        out_specs=[vmem] * 5,
        out_shape=[jax.ShapeDtypeStruct((4, 2, 32, 256), BF16)] * 4 + [jax.ShapeDtypeStruct((2, 4, 4, 32, 256), BF16)],
        scratch_shapes=[pltpu.SemaphoreType.DMA((20,))],
        cost_estimate=pl.CostEstimate(flops=0, bytes_accessed=2097152, transcendentals=0),
        compiler_params=pltpu.CompilerParams(vmem_limit_bytes=8 * 1024 * 1024),
        name="pack",
    )(where.astype(jnp.int32), projections.reshape(4, 8, 2, 32, 256))


def finish_kernel(where_ref, *refs):
    near_ref, far_refs, (a_ref, fwd_ref, rinv_ref, col_ref, res_ref, part_ref, held_ref) = refs[0], refs[1:5], refs[5:]
    dh, dl, own_y = where_ref[0], where_ref[1], where_ref[2]
    for b in range(4):
        g = dl ^ b
        for a in range(2):
            zh = dh ^ (dl & 1) ^ a
            for t in range(2):
                rinv = rinv_ref[g, 0:1, t * 256 : (t + 1) * 256]
                for y in range(4):
                    rows = pl.ds(pl.multiple_of((y * 2 + zh) * 32, 32), 32)
                    lanes = slice(t * 256, (t + 1) * 256)
                    block = near_ref[(y ^ own_y) * 2 + t, b] if a == 0 else far_refs[b][t * 4 + y]
                    res = ((block.astype(F32) - fwd_ref[g, rows, lanes]) * rinv).astype(BF16)
                    res_ref[g * 2 + t, rows, :] = res
                    held_ref[rows, lanes] = res
        for q in range(4):
            add = contract(held_ref[...], a_ref[g, q * 256 : (q + 1) * 256, :], 1, 1)
            if b == 0:
                part_ref[q, 0:256, :] = add
            else:
                part_ref[q, 0:256, :] += add
    for q in range(4):
        part_ref[q, 256:264, :] = col_ref[:, q * 256 : (q + 1) * 256]


def finish(where, near, far, a, fwd, rinv, col):
    vmem = pl.BlockSpec(memory_space=pltpu.VMEM)
    return pl.pallas_call(
        finish_kernel,
        in_specs=[pl.BlockSpec(memory_space=pltpu.SMEM)] + [vmem] * 9,
        out_specs=[vmem, vmem],
        out_shape=[
            jax.ShapeDtypeStruct((8, 256, 256), BF16),
            jax.ShapeDtypeStruct((4, 264, 256), F32),
        ],
        scratch_shapes=[pltpu.VMEM((256, 512), BF16)],
        cost_estimate=pl.CostEstimate(flops=1100000000, bytes_accessed=10000000, transcendentals=0),
        compiler_params=pltpu.CompilerParams(vmem_limit_bytes=40 * 1024 * 1024),
        name="finish",
    )(where, near, *far, a, fwd, rinv, col)


def on_device(projections, start_image, system, first_tile):
    x, zl, y, zh = (lax.axis_index(name) for name in ("x", "zl", "y", "zh"))
    dh, dl = zl // 4, zl % 4
    def send(block, half, b):
        def dest(x, zl, core, y, zh):
            low = (zl % 4) ^ b
            return (x ^ y, (zh ^ (low & 1) ^ half) * 4 + low, core, x, zl // 4)

        return lax.ppermute(block, AXES, pairs(dest))

    *near, far = pack(jnp.stack([x, dl, zh]), projections)
    first_tile, image, system, far = lax.optimization_barrier((first_tile, start_image, system, far))
    near = [send(block.reshape(8, 32, 256), 0, b) for b, block in enumerate(near)]
    far = lax.all_to_all(far.reshape(8, 4, 32, 256), ("core", "y"), 0, 0, tiled=True)
    near, _ = lax.optimization_barrier((near, far))
    far = [lax.dynamic_index_in_dim(far, dl ^ b, 1, keepdims=False) for b in range(4)]
    near = jnp.stack(near, 1)
    far = [send(block, 1, b) for b, block in enumerate(far)]
    near = lax.all_to_all(near, ("x", "core"), 0, 0, tiled=True)
    a, fwd, rinv, col = prepare(first_tile, image, system)
    where = jnp.stack([dh, dl, y]).astype(jnp.int32)
    residual, part = finish(where, near, far, a, fwd, rinv, col)
    part = lax.all_to_all(part, "y", 0, 0, tiled=True).sum(0)
    halves = jnp.stack([part[:, :128], part[:, 128:]])
    mine = lax.dynamic_index_in_dim(halves, zh, 0, keepdims=False)
    other = lax.dynamic_index_in_dim(halves, 1 - zh, 0, keepdims=False)
    swap = pairs(lambda x, zl, core, y, zh: (x, zl, core, y, 1 - zh))
    total = mine + lax.ppermute(other, AXES, swap)
    local = lax.dynamic_slice_in_dim(start_image, (y * 2 + zh) * 128, 128, 1).astype(F32)
    new_image = local + total[:256] / total[256:257]
    return new_image, residual


def solution(mesh):
    mesh = Mesh(mesh.devices.reshape(SIZES), AXES)
    cuts, ang = ("x", "zl", "core"), ("y", "zh")
    in_specs = (
        P(cuts, None, ang, None, None),
        P(cuts, None),
        P(ang, None, None, None, None),
        P(ang, None),
    )
    out_specs = (P(cuts, ang), P(ang, cuts, None))
    return jax.shard_map(on_device, mesh=mesh, in_specs=in_specs, out_specs=out_specs, check_vma=False)
```

```python
import functools

import jax
import jax.numpy as jnp
from jax import lax
from jax.experimental import pallas as pl
from jax.experimental.pallas import tpu as pltpu
from jax.sharding import Mesh
from jax.sharding import PartitionSpec as P

AXES = ("x", "zl", "core", "y", "zh")
SIZES = (4, 8, 2, 4, 2)
HALVES = 2
HALF = 32 // HALVES
F32 = jnp.float32
BF16 = jnp.bfloat16


def index_of(x, zl, core, y, zh):
    return (((x * 8 + zl) * 2 + core) * 4 + y) * 2 + zh


def pairs(dest):
    out = []
    for x in range(4):
        for zl in range(8):
            for core in range(2):
                for y in range(4):
                    for zh in range(2):
                        out.append((index_of(x, zl, core, y, zh), index_of(*dest(x, zl, core, y, zh))))
    return out


def contract(a, b, da, db):
    return lax.dot_general(a, b, (((da,), (db,)), ((), ())), preferred_element_type=F32)


def prepare_kernel(first_ref, image_ref, system_ref, a_ref, fwd_ref, rinv_ref, col_ref):
    g = pl.program_id(0)
    low = lax.broadcasted_iota(jnp.int32, (64, 128), 1) < 64
    for p in range(16):
        f = first_ref[g, p]
        t0 = system_ref[0, p, 0].astype(F32)
        t1 = system_ref[0, p, 1].astype(F32)
        even = f % 2 == 0
        e = jnp.where(even, t0, t1)
        o = jnp.where(even, t1, t0)
        x0 = jnp.where(low, e, pltpu.roll(o, 64, 1))
        x1 = jnp.where(low, pltpu.roll(e, 64, 1), o)
        ve = jnp.where((f == 1) | (f == 2), 1, 0)
        vo = jnp.where(f >= 2, 1, 0)
        place = jnp.where(low, ve, vo)
        for t, xt in ((0, x0), (1, x1)):
            for v in range(2):
                a_ref[0, p * 64 : (p + 1) * 64, t * 256 + v * 128 : t * 256 + (v + 1) * 128] = jnp.where(
                    place == v, xt, 0.0
                ).astype(BF16)
    a = a_ref[0]
    fwd_ref[0] = contract(image_ref[...], a, 1, 0)
    rows = contract(jnp.ones((8, 1024), BF16), a, 1, 0)
    rinv_ref[0] = 1.0 / rows
    cols = contract(jnp.ones((8, 512), BF16), a, 1, 1)

    @pl.when(g == 0)
    def _():
        col_ref[...] = cols

    @pl.when(g > 0)
    def _():
        col_ref[...] += cols


def prepare(first, image, system):
    return pl.pallas_call(
        prepare_kernel,
        grid=(4,),
        in_specs=[
            pl.BlockSpec(memory_space=pltpu.SMEM),
            pl.BlockSpec((256, 1024), lambda g: (0, 0)),
            pl.BlockSpec((1, 16, 2, 64, 128), lambda g: (g, 0, 0, 0, 0)),
        ],
        out_specs=[
            pl.BlockSpec((1, 1024, 512), lambda g: (g, 0, 0)),
            pl.BlockSpec((1, 256, 512), lambda g: (g, 0, 0)),
            pl.BlockSpec((1, 8, 512), lambda g: (g, 0, 0)),
            pl.BlockSpec((8, 1024), lambda g: (0, 0)),
        ],
        out_shape=[
            jax.ShapeDtypeStruct((4, 1024, 512), BF16),
            jax.ShapeDtypeStruct((4, 256, 512), F32),
            jax.ShapeDtypeStruct((4, 8, 512), F32),
            jax.ShapeDtypeStruct((8, 1024), F32),
        ],
        cost_estimate=pl.CostEstimate(flops=1100000000, bytes_accessed=10000000, transcendentals=0),
        compiler_params=pltpu.CompilerParams(vmem_limit_bytes=40 * 1024 * 1024),
        name="prepare",
    )(first, image, system)


def pack_kernel(where_ref, p_ref, *refs):
    l, zh = where_ref[0], where_ref[1]
    sems = refs[HALVES]
    copies = []
    for half in range(HALVES):
        rows = pl.ds(half * HALF, HALF)
        for slot in range(8):
            zl = (zh ^ (slot // 4)) * 4 + ((slot % 4 - l) & 3)
            copies.append(pltpu.make_async_copy(p_ref.at[:, zl, :, rows], refs[half].at[slot], sems.at[half * 8 + slot]))
    for copy in copies:
        copy.start()
    for copy in copies:
        copy.wait()


def pack(where, projections):
    return pl.pallas_call(
        pack_kernel,
        in_specs=[pl.BlockSpec(memory_space=pltpu.SMEM), pl.BlockSpec(memory_space=pl.ANY)],
        out_specs=[pl.BlockSpec(memory_space=pltpu.VMEM)] * HALVES,
        out_shape=[jax.ShapeDtypeStruct((8, 4, 2, HALF, 256), BF16)] * HALVES,
        scratch_shapes=[pltpu.SemaphoreType.DMA((8 * HALVES,))],
        cost_estimate=pl.CostEstimate(flops=0, bytes_accessed=2097152, transcendentals=0),
        compiler_params=pltpu.CompilerParams(vmem_limit_bytes=8 * 1024 * 1024),
        name="pack",
    )(where, projections.reshape(4, 8, 2, 32, 256))


def finish_kernel(where_ref, *refs):
    parts, (a_ref, fwd_ref, rinv_ref, col_ref, res_ref, part_ref, held_ref) = refs[:HALVES], refs[HALVES:]
    dh, dl, own_y = where_ref[0], where_ref[1], where_ref[2]
    for b in range(4):
        g = (b - dl) & 3
        slot = (b ^ own_y) * 2
        for t in range(2):
            lanes = slice(t * 256, (t + 1) * 256)
            rinv = rinv_ref[g, 0:1, lanes]
            for a in range(2):
                for y in range(4):
                    for half in range(HALVES):
                        start = (y * 2 + (dh ^ a)) * 32 + half * HALF
                        rows = pl.ds(pl.multiple_of(start, HALF), HALF)
                        block = parts[half][slot + a, t * 4 + y].astype(F32)
                        res = ((block - fwd_ref[g, rows, lanes]) * rinv).astype(BF16)
                        res_ref[g * 2 + t, rows, :] = res
                        held_ref[rows, lanes] = res
        for q in range(4):
            add = contract(held_ref[...], a_ref[g, q * 256 : (q + 1) * 256, :], 1, 1)
            if b == 0:
                part_ref[q, 0:256, :] = add
            else:
                part_ref[q, 0:256, :] += add
    for q in range(4):
        part_ref[q, 256:264, :] = col_ref[:, q * 256 : (q + 1) * 256]


def finish(where, parts, a, fwd, rinv, col):
    vmem = pl.BlockSpec(memory_space=pltpu.VMEM)
    return pl.pallas_call(
        finish_kernel,
        in_specs=[pl.BlockSpec(memory_space=pltpu.SMEM)] + [vmem] * (HALVES + 4),
        out_specs=[vmem, vmem],
        out_shape=[
            jax.ShapeDtypeStruct((8, 256, 256), BF16),
            jax.ShapeDtypeStruct((4, 264, 256), F32),
        ],
        scratch_shapes=[pltpu.VMEM((256, 512), BF16)],
        cost_estimate=pl.CostEstimate(flops=1100000000, bytes_accessed=10000000, transcendentals=0),
        compiler_params=pltpu.CompilerParams(vmem_limit_bytes=40 * 1024 * 1024),
        name="finish",
    )(where, *parts, a, fwd, rinv, col)


def on_device(projections, start_image, system, first_tile):
    zl, y, zh = (lax.axis_index(name) for name in ("zl", "y", "zh"))
    dh, dl = zl // 4, zl % 4
    def dest(x, zl, core, y, zh):
        return (x ^ y, (zh ^ core) * 4 + ((y - zl % 4) & 3), core, x, zl // 4)

    parts = []
    packed = pack(jnp.stack([dl, zh]), projections)
    first_tile, image, system, packed = lax.optimization_barrier((first_tile, start_image, system, packed))
    for part in packed:
        part = part.reshape(8, 8, HALF, 256)
        if parts:
            part, parts[-1] = lax.optimization_barrier((part, parts[-1]))
        parts.append(lax.all_to_all(part, ("core", "y"), 0, 0, tiled=True))
    parts = [lax.ppermute(part.swapaxes(0, 1), AXES, pairs(dest)) for part in parts]
    for n in range(HALVES):
        if n:
            parts[n], parts[n - 1] = lax.optimization_barrier((parts[n], parts[n - 1]))
        parts[n] = lax.all_to_all(parts[n], ("x", "core"), 0, 0, tiled=True)
    a, fwd, rinv, col = prepare(first_tile, image, system)
    where = jnp.stack([dh, dl, y]).astype(jnp.int32)
    residual, part = finish(where, parts, a, fwd, rinv, col)
    part = lax.all_to_all(part, "y", 0, 0, tiled=True).sum(0)
    halves = jnp.stack([part[:, :128], part[:, 128:]])
    mine = lax.dynamic_index_in_dim(halves, zh, 0, keepdims=False)
    other = lax.dynamic_index_in_dim(halves, 1 - zh, 0, keepdims=False)
    swap = pairs(lambda x, zl, core, y, zh: (x, zl, core, y, 1 - zh))
    total = mine + lax.ppermute(other, AXES, swap)
    local = lax.dynamic_slice_in_dim(start_image, (y * 2 + zh) * 128, 128, 1).astype(F32)
    new_image = local + total[:256] / total[256:257]
    return new_image, residual


def solution(mesh):
    mesh = Mesh(mesh.devices.reshape(SIZES), AXES)
    cuts, ang = ("x", "zl", "core"), ("y", "zh")
    in_specs = (
        P(cuts, None, ang, None, None),
        P(cuts, None),
        P(ang, None, None, None, None),
        P(ang, None),
    )
    out_specs = (P(cuts, ang), P(ang, cuts, None))
    return jax.shard_map(on_device, mesh=mesh, in_specs=in_specs, out_specs=out_specs, check_vma=False)
```

```python
import functools

import jax
import jax.numpy as jnp
from jax import lax
from jax.experimental import pallas as pl
from jax.experimental.pallas import tpu as pltpu
from jax.sharding import Mesh
from jax.sharding import PartitionSpec as P

AXES = ("x", "zl", "core", "y", "zh")
SIZES = (4, 8, 2, 4, 2)
HALVES = 2
HALF = 32 // HALVES
VMEM_LIMIT = 60 * 1024 * 1024
F32 = jnp.float32
BF16 = jnp.bfloat16


def index_of(x, zl, core, y, zh):
    return (((x * 8 + zl) * 2 + core) * 4 + y) * 2 + zh


def pairs(dest):
    out = []
    for x in range(4):
        for zl in range(8):
            for core in range(2):
                for y in range(4):
                    for zh in range(2):
                        out.append((index_of(x, zl, core, y, zh), index_of(*dest(x, zl, core, y, zh))))
    return out


def contract(a, b, da, db):
    return lax.dot_general(a, b, (((da,), (db,)), ((), ())), preferred_element_type=F32)


def prepare_kernel(first_ref, image_ref, system_ref, a_ref, fwd_ref, rinv_ref, col_ref):
    g = pl.program_id(0)
    low = lax.broadcasted_iota(jnp.int32, (64, 128), 1) < 64
    for p in range(16):
        f = first_ref[g, p]
        t0 = system_ref[0, p, 0].astype(F32)
        t1 = system_ref[0, p, 1].astype(F32)
        even = f % 2 == 0
        e = jnp.where(even, t0, t1)
        o = jnp.where(even, t1, t0)
        x0 = jnp.where(low, e, pltpu.roll(o, 64, 1))
        x1 = jnp.where(low, pltpu.roll(e, 64, 1), o)
        ve = jnp.where((f == 1) | (f == 2), 1, 0)
        vo = jnp.where(f >= 2, 1, 0)
        place = jnp.where(low, ve, vo)
        for t, xt in ((0, x0), (1, x1)):
            for v in range(2):
                a_ref[0, p * 64 : (p + 1) * 64, t * 256 + v * 128 : t * 256 + (v + 1) * 128] = jnp.where(
                    place == v, xt, 0.0
                ).astype(BF16)
    a = a_ref[0]
    fwd_ref[0] = contract(image_ref[...], a, 1, 0)
    rows = contract(jnp.ones((8, 1024), BF16), a, 1, 0)
    rinv_ref[0] = 1.0 / rows
    cols = contract(jnp.ones((8, 512), BF16), a, 1, 1)

    @pl.when(g == 0)
    def _():
        col_ref[...] = cols

    @pl.when(g > 0)
    def _():
        col_ref[...] += cols


def prepare(first, image, system):
    return pl.pallas_call(
        prepare_kernel,
        grid=(4,),
        in_specs=[
            pl.BlockSpec(memory_space=pltpu.SMEM),
            pl.BlockSpec((256, 1024), lambda g: (0, 0)),
            pl.BlockSpec((1, 16, 2, 64, 128), lambda g: (g, 0, 0, 0, 0)),
        ],
        out_specs=[
            pl.BlockSpec((1, 1024, 512), lambda g: (g, 0, 0)),
            pl.BlockSpec((1, 256, 512), lambda g: (g, 0, 0)),
            pl.BlockSpec((1, 8, 512), lambda g: (g, 0, 0)),
            pl.BlockSpec((8, 1024), lambda g: (0, 0)),
        ],
        out_shape=[
            jax.ShapeDtypeStruct((4, 1024, 512), BF16),
            jax.ShapeDtypeStruct((4, 256, 512), F32),
            jax.ShapeDtypeStruct((4, 8, 512), F32),
            jax.ShapeDtypeStruct((8, 1024), F32),
        ],
        cost_estimate=pl.CostEstimate(flops=1100000000, bytes_accessed=10000000, transcendentals=0),
        compiler_params=pltpu.CompilerParams(vmem_limit_bytes=VMEM_LIMIT),
        name="prepare",
    )(first, image, system)


def pack_kernel(where_ref, p_ref, *refs):
    l, zh = where_ref[0], where_ref[1]
    sems = refs[HALVES]
    copies = []
    for half in range(HALVES):
        rows = pl.ds(half * HALF, HALF)
        for slot in range(8):
            zl = (zh ^ (slot // 4)) * 4 + ((((slot % 4) ^ half) - l) & 3)
            copies.append(pltpu.make_async_copy(p_ref.at[:, zl, :, rows], refs[half].at[slot], sems.at[half * 8 + slot]))
    for copy in copies:
        copy.start()
    for copy in copies:
        copy.wait()


def pack(where, projections):
    return pl.pallas_call(
        pack_kernel,
        in_specs=[pl.BlockSpec(memory_space=pltpu.SMEM), pl.BlockSpec(memory_space=pl.ANY)],
        out_specs=[pl.BlockSpec(memory_space=pltpu.VMEM)] * HALVES,
        out_shape=[jax.ShapeDtypeStruct((8, 4, 2, HALF, 256), BF16)] * HALVES,
        scratch_shapes=[pltpu.SemaphoreType.DMA((8 * HALVES,))],
        cost_estimate=pl.CostEstimate(flops=0, bytes_accessed=2097152, transcendentals=0),
        compiler_params=pltpu.CompilerParams(vmem_limit_bytes=VMEM_LIMIT),
        name="pack",
    )(where, projections.reshape(4, 8, 2, 32, 256))


def finish_kernel(where_ref, *refs):
    parts, (a_ref, fwd_ref, rinv_ref, col_ref, res_ref, part_ref, held_ref) = refs[:HALVES], refs[HALVES:]
    dh, dl, own_y = where_ref[0], where_ref[1], where_ref[2]
    g = pl.program_id(0)
    b = (g + dl) & 3
    for t in range(2):
        lanes = slice(t * 256, (t + 1) * 256)
        rinv = rinv_ref[0, 0:1, lanes]
        for a in range(2):
            for y in range(4):
                for half in range(HALVES):
                    start = (y * 2 + (dh ^ a)) * 32 + half * HALF
                    rows = pl.ds(pl.multiple_of(start, HALF), HALF)
                    block = parts[half][(b ^ half ^ own_y) * 2 + a, t * 4 + y].astype(F32)
                    res = ((block - fwd_ref[0, rows, lanes]) * rinv).astype(BF16)
                    res_ref[t, rows, :] = res
                    held_ref[rows, lanes] = res
    adds = [contract(held_ref[...], a_ref[0, q * 256 : (q + 1) * 256, :], 1, 1) for q in range(4)]

    @pl.when(g == 0)
    def _():
        row = lax.broadcasted_iota(jnp.int32, (16, 256), 0)
        for q in range(4):
            part_ref[q, 0:256, :] = adds[q]
            cols = col_ref[0:1, q * 256 : (q + 1) * 256]
            high = cols.astype(BF16).astype(F32)
            part_ref[q, 256:272, :] = jnp.where(row == 0, high, jnp.where(row == 1, cols - high, 0.0))

    @pl.when(g > 0)
    def _():
        for q in range(4):
            part_ref[q, 0:256, :] += adds[q]


def finish(where, parts, a, fwd, rinv, col):
    return pl.pallas_call(
        finish_kernel,
        grid=(4,),
        in_specs=[pl.BlockSpec(memory_space=pltpu.SMEM)]
        + [pl.BlockSpec((8, 8, HALF, 256), lambda g: (0, 0, 0, 0))] * HALVES
        + [
            pl.BlockSpec((1, 1024, 512), lambda g: (g, 0, 0)),
            pl.BlockSpec((1, 256, 512), lambda g: (g, 0, 0)),
            pl.BlockSpec((1, 8, 512), lambda g: (g, 0, 0)),
            pl.BlockSpec((8, 1024), lambda g: (0, 0)),
        ],
        out_specs=[
            pl.BlockSpec((2, 256, 256), lambda g: (g, 0, 0)),
            pl.BlockSpec((4, 272, 256), lambda g: (0, 0, 0)),
        ],
        out_shape=[
            jax.ShapeDtypeStruct((8, 256, 256), BF16),
            jax.ShapeDtypeStruct((4, 272, 256), F32),
        ],
        scratch_shapes=[pltpu.VMEM((256, 512), BF16)],
        cost_estimate=pl.CostEstimate(flops=1100000000, bytes_accessed=10000000, transcendentals=0),
        compiler_params=pltpu.CompilerParams(vmem_limit_bytes=VMEM_LIMIT),
        name="finish",
    )(where, *parts, a, fwd, rinv, col)


def on_device(projections, start_image, system, first_tile):
    zl, y, zh = (lax.axis_index(name) for name in ("zl", "y", "zh"))
    dh, dl = zl // 4, zl % 4
    def send(part, half):
        def dest(x, zl, core, y, zh):
            return (x ^ y, (zh ^ core) * 4 + (((y ^ half) - zl % 4) & 3), core, x, zl // 4)

        return lax.ppermute(part, AXES, pairs(dest))

    parts = []
    packed = pack(jnp.stack([dl, zh]), projections)
    first_tile, image, system, packed = lax.optimization_barrier((first_tile, start_image, system, packed))
    for part in packed:
        part = part.reshape(8, 8, HALF, 256)
        if parts:
            part, parts[-1] = lax.optimization_barrier((part, parts[-1]))
        parts.append(lax.all_to_all(part, ("core", "y"), 0, 0, tiled=True))
    parts = [send(part.swapaxes(0, 1), half) for half, part in enumerate(parts)]
    a, fwd, rinv, col = prepare(first_tile, image, system)
    parts[0], col = lax.optimization_barrier((parts[0], col))
    for n in range(HALVES):
        if n:
            parts[n], parts[n - 1] = lax.optimization_barrier((parts[n], parts[n - 1]))
        parts[n] = lax.all_to_all(parts[n], ("x", "core"), 0, 0, tiled=True)
    where = jnp.stack([dh, dl, y]).astype(jnp.int32)
    residual, part = finish(where, parts, a, fwd, rinv, col)
    part = lax.all_to_all(part.astype(jnp.float16), "y", 0, 0, tiled=True).astype(F32).sum(0)
    halves = jnp.stack([part[:, :128], part[:, 128:]])
    mine = lax.dynamic_index_in_dim(halves, zh, 0, keepdims=False)
    other = lax.dynamic_index_in_dim(halves, 1 - zh, 0, keepdims=False)
    cols = other[256:257] + other[257:258]
    high = lax.reduce_precision(cols, 8, 7)
    other = jnp.concatenate([other[:256], high, cols - high, jnp.zeros((14, 128), F32)]).astype(jnp.float16)
    swap = pairs(lambda x, zl, core, y, zh: (x, zl, core, y, 1 - zh))
    total = mine + lax.ppermute(other, AXES, swap).astype(F32)
    local = lax.dynamic_slice_in_dim(start_image, (y * 2 + zh) * 128, 128, 1).astype(F32)
    new_image = local + total[:256] / (total[256:257] + total[257:258])
    return new_image, residual


def solution(mesh):
    mesh = Mesh(mesh.devices.reshape(SIZES), AXES)
    cuts, ang = ("x", "zl", "core"), ("y", "zh")
    in_specs = (
        P(cuts, None, ang, None, None),
        P(cuts, None),
        P(ang, None, None, None, None),
        P(ang, None),
    )
    out_specs = (P(cuts, ang), P(ang, cuts, None))
    return jax.shard_map(on_device, mesh=mesh, in_specs=in_specs, out_specs=out_specs, check_vma=False)
```

```python
import functools

import jax
import jax.numpy as jnp
from jax import lax
from jax.experimental import pallas as pl
from jax.experimental.pallas import tpu as pltpu
from jax.sharding import Mesh
from jax.sharding import PartitionSpec as P

AXES = ("x", "zl", "core", "y", "zh")
SIZES = (4, 8, 2, 4, 2)
HALVES = 2
HALF = 32 // HALVES
VMEM_LIMIT = 60 * 1024 * 1024
F32 = jnp.float32
BF16 = jnp.bfloat16


def index_of(x, zl, core, y, zh):
    return (((x * 8 + zl) * 2 + core) * 4 + y) * 2 + zh


def pairs(dest):
    out = []
    for x in range(4):
        for zl in range(8):
            for core in range(2):
                for y in range(4):
                    for zh in range(2):
                        out.append((index_of(x, zl, core, y, zh), index_of(*dest(x, zl, core, y, zh))))
    return out


def contract(a, b, da, db):
    return lax.dot_general(a, b, (((da,), (db,)), ((), ())), preferred_element_type=F32)


def prepare_kernel(first_ref, image_ref, system_ref, a_ref, fwd_ref, rinv_ref, col_ref):
    g = pl.program_id(0)
    low = lax.broadcasted_iota(jnp.int32, (64, 128), 1) < 64
    for p in range(16):
        f = first_ref[g, p]
        t0 = system_ref[0, p, 0].astype(F32)
        t1 = system_ref[0, p, 1].astype(F32)
        even = f % 2 == 0
        e = jnp.where(even, t0, t1)
        o = jnp.where(even, t1, t0)
        x0 = jnp.where(low, e, pltpu.roll(o, 64, 1))
        x1 = jnp.where(low, pltpu.roll(e, 64, 1), o)
        ve = jnp.where((f == 1) | (f == 2), 1, 0)
        vo = jnp.where(f >= 2, 1, 0)
        place = jnp.where(low, ve, vo)
        for t, xt in ((0, x0), (1, x1)):
            for v in range(2):
                a_ref[0, p * 64 : (p + 1) * 64, t * 256 + v * 128 : t * 256 + (v + 1) * 128] = jnp.where(
                    place == v, xt, 0.0
                ).astype(BF16)
    a = a_ref[0]
    fwd = contract(image_ref[...], a, 1, 0)
    for half in range(HALVES):
        for group in range(8):
            start = group * 32 + half * HALF
            fwd_ref[0, half, group * HALF : (group + 1) * HALF, :] = fwd[start : start + HALF, :]
    rows = contract(jnp.ones((8, 1024), BF16), a, 1, 0)
    rinv_ref[0] = 1.0 / rows
    cols = contract(jnp.ones((8, 512), BF16), a, 1, 1)

    @pl.when(g == 0)
    def _():
        col_ref[...] = cols

    @pl.when(g > 0)
    def _():
        col_ref[...] += cols


def prepare(first, image, system):
    return pl.pallas_call(
        prepare_kernel,
        grid=(4,),
        in_specs=[
            pl.BlockSpec(memory_space=pltpu.SMEM),
            pl.BlockSpec((256, 1024), lambda g: (0, 0)),
            pl.BlockSpec((1, 16, 2, 64, 128), lambda g: (g, 0, 0, 0, 0)),
        ],
        out_specs=[
            pl.BlockSpec((1, 1024, 512), lambda g: (g, 0, 0)),
            pl.BlockSpec((1, HALVES, 8 * HALF, 512), lambda g: (g, 0, 0, 0)),
            pl.BlockSpec((1, 8, 512), lambda g: (g, 0, 0)),
            pl.BlockSpec((8, 1024), lambda g: (0, 0)),
        ],
        out_shape=[
            jax.ShapeDtypeStruct((4, 1024, 512), BF16),
            jax.ShapeDtypeStruct((4, HALVES, 8 * HALF, 512), F32),
            jax.ShapeDtypeStruct((4, 8, 512), F32),
            jax.ShapeDtypeStruct((8, 1024), F32),
        ],
        cost_estimate=pl.CostEstimate(flops=100000, bytes_accessed=100000, transcendentals=0),
        compiler_params=pltpu.CompilerParams(vmem_limit_bytes=VMEM_LIMIT),
        name="prepare",
    )(first, image, system)


def pack_kernel(where_ref, p_ref, *refs):
    l, zh = where_ref[0], where_ref[1]
    sems = refs[HALVES]
    copies = []
    for half in range(HALVES):
        rows = pl.ds(half * HALF, HALF)
        for slot in range(8):
            zl = (zh ^ (slot // 4)) * 4 + ((((slot % 4) ^ half) - l) & 3)
            copies.append(pltpu.make_async_copy(p_ref.at[:, zl, :, rows], refs[half].at[slot], sems.at[half * 8 + slot]))
    for copy in copies:
        copy.start()
    for copy in copies:
        copy.wait()


def pack(where, projections):
    return pl.pallas_call(
        pack_kernel,
        in_specs=[pl.BlockSpec(memory_space=pltpu.SMEM), pl.BlockSpec(memory_space=pl.ANY)],
        out_specs=[pl.BlockSpec(memory_space=pltpu.VMEM)] * HALVES,
        out_shape=[jax.ShapeDtypeStruct((8, 4, 2, HALF, 256), BF16)] * HALVES,
        scratch_shapes=[pltpu.SemaphoreType.DMA((8 * HALVES,))],
        cost_estimate=pl.CostEstimate(flops=0, bytes_accessed=2097152, transcendentals=0),
        compiler_params=pltpu.CompilerParams(vmem_limit_bytes=VMEM_LIMIT),
        name="pack",
    )(where, projections.reshape(4, 8, 2, 32, 256))


def finish_kernel(half, where_ref, chunk_ref, a_hbm, fwd_hbm, rinv_ref, col_ref, *refs):
    res_hbm, part_hbm, a_ref, fwd_ref, res_ref, held_ref, part_ref, sems = refs[-8:]
    dh, dl, own_y = where_ref[0], where_ref[1], where_ref[2]
    copies = []
    for g in range(4):
        copies.append(pltpu.make_async_copy(fwd_hbm.at[g, half], fwd_ref.at[g], sems.at[g]))
    for g in range(4):
        copies.append(pltpu.make_async_copy(a_hbm.at[g], a_ref.at[g], sems.at[4 + g]))
    for copy in copies:
        copy.start()
    for g in range(4):
        b = (g + dl) & 3
        copies[g].wait()
        for t in range(2):
            lanes = slice(t * 256, (t + 1) * 256)
            rinv = rinv_ref[g, 0:1, lanes]
            for a in range(2):
                for y in range(4):
                    group = y * 2 + (dh ^ a)
                    rows = pl.ds(pl.multiple_of(group * HALF, HALF), HALF)
                    block = chunk_ref[(b ^ half ^ own_y) * 2 + a, t * 4 + y].astype(F32)
                    res = ((block - fwd_ref[g, rows, lanes]) * rinv).astype(BF16)
                    res_ref[g * 2 + t, group] = res
                    held_ref[g, rows, lanes] = res
    out = pltpu.make_async_copy(res_ref, res_hbm.at[:, :, pl.ds(half * HALF, HALF)], sems.at[8])
    out.start()
    for copy in copies[4:]:
        copy.wait()
    for q in range(4):
        total = contract(held_ref[0], a_ref[0, q * 256 : (q + 1) * 256, :], 1, 1)
        for g in range(1, 4):
            total += contract(held_ref[g], a_ref[g, q * 256 : (q + 1) * 256, :], 1, 1)
        part_ref[q, 0 : 8 * HALF, :] = total
        if half == 0:
            row = lax.broadcasted_iota(jnp.int32, (16, 256), 0)
            cols = col_ref[0:1, q * 256 : (q + 1) * 256]
            high = cols.astype(BF16).astype(F32)
            part_ref[q, 8 * HALF :, :] = jnp.where(row == 0, high, jnp.where(row == 1, cols - high, 0.0))
    shares = [pltpu.make_async_copy(part_ref.at[:, 0 : 8 * HALF], part_hbm.at[:, pl.ds(half * 8 * HALF, 8 * HALF)], sems.at[9])]
    if half == 0:
        shares.append(pltpu.make_async_copy(part_ref.at[:, 8 * HALF :], part_hbm.at[:, 256:272], sems.at[10]))
    for share in shares:
        share.start()
    for share in shares:
        share.wait()
    out.wait()


def finish(half, where, chunk, a, fwd, rinv, col, before=()):
    vmem, hbm = pl.BlockSpec(memory_space=pltpu.VMEM), pl.BlockSpec(memory_space=pl.ANY)
    return pl.pallas_call(
        functools.partial(finish_kernel, half),
        in_specs=[pl.BlockSpec(memory_space=pltpu.SMEM), vmem, hbm, hbm, vmem, vmem] + [hbm] * len(before),
        out_specs=[hbm, hbm],
        out_shape=[
            jax.ShapeDtypeStruct((8, 8, 32, 256), BF16),
            jax.ShapeDtypeStruct((4, 272, 256), F32),
        ],
        scratch_shapes=[
            pltpu.VMEM((4, 1024, 512), BF16),
            pltpu.VMEM((4, 8 * HALF, 512), F32),
            pltpu.VMEM((8, 8, HALF, 256), BF16),
            pltpu.VMEM((4, 8 * HALF, 512), BF16),
            pltpu.VMEM((4, 8 * HALF + (16 if half == 0 else 0), 256), F32),
            pltpu.SemaphoreType.DMA((11,)),
        ],
        input_output_aliases={6: 0, 7: 1} if before else {},
        cost_estimate=pl.CostEstimate(flops=550000000, bytes_accessed=8000000, transcendentals=0),
        compiler_params=pltpu.CompilerParams(vmem_limit_bytes=VMEM_LIMIT),
        name=("finish_first", "finish_second")[half],
    )(where, chunk, a, fwd, rinv, col, *before)


def on_device(projections, start_image, system, first_tile):
    zl, y, zh = (lax.axis_index(name) for name in ("zl", "y", "zh"))
    dh, dl = zl // 4, zl % 4
    def send(part, half):
        def dest(x, zl, core, y, zh):
            return (x ^ y, (zh ^ core) * 4 + (((y ^ half) - zl % 4) & 3), core, x, zl // 4)

        return lax.ppermute(part, AXES, pairs(dest))

    where = jnp.stack([dh, dl, y]).astype(jnp.int32)
    first, second = pack(jnp.stack([dl, zh]), projections)
    first = lax.all_to_all(first.reshape(8, 8, HALF, 256), ("core", "y"), 0, 0, tiled=True)
    second, first = lax.optimization_barrier((second, first))
    second = lax.all_to_all(second.reshape(8, 8, HALF, 256), ("core", "y"), 0, 0, tiled=True)
    first = send(first.swapaxes(0, 1), 0)
    first_tile, image, system, second = lax.optimization_barrier((first_tile, start_image, system, second))
    a, fwd, rinv, col = prepare(first_tile, image, system)
    second, col = lax.optimization_barrier((second, col))
    second = send(second.swapaxes(0, 1), 1)
    first, _ = lax.optimization_barrier((first, col))

    first = lax.all_to_all(first, ("x", "core"), 0, 0, tiled=True)
    second, first = lax.optimization_barrier((second, first))
    done = finish(0, where, first, a, fwd, rinv, col)
    second = lax.all_to_all(second, ("x", "core"), 0, 0, tiled=True)
    residual, part = finish(1, where, second, a, fwd, rinv, col, done)

    part = lax.all_to_all(part.astype(jnp.float16), "y", 0, 0, tiled=True).astype(F32).sum(0)
    halves = jnp.stack([part[:, :128], part[:, 128:]])
    mine = lax.dynamic_index_in_dim(halves, zh, 0, keepdims=False)
    other = lax.dynamic_index_in_dim(halves, 1 - zh, 0, keepdims=False)
    cols = other[256:257] + other[257:258]
    high = lax.reduce_precision(cols, 8, 7)
    other = jnp.concatenate([other[:256], high, cols - high, jnp.zeros((14, 128), F32)]).astype(jnp.float16)
    swap = pairs(lambda x, zl, core, y, zh: (x, zl, core, y, 1 - zh))
    total = mine + lax.ppermute(other, AXES, swap).astype(F32)
    update = total[:256] * (1.0 / (total[256:257] + total[257:258]))
    update = update.reshape(HALVES, 8, HALF, 128).swapaxes(0, 1).reshape(256, 128)
    local = lax.dynamic_slice_in_dim(start_image, (y * 2 + zh) * 128, 128, 1).astype(F32)
    return local + update, residual.reshape(8, 256, 256)


def solution(mesh):
    mesh = Mesh(mesh.devices.reshape(SIZES), AXES)
    cuts, ang = ("x", "zl", "core"), ("y", "zh")
    in_specs = (
        P(cuts, None, ang, None, None),
        P(cuts, None),
        P(ang, None, None, None, None),
        P(ang, None),
    )
    out_specs = (P(cuts, ang), P(ang, cuts, None))
    return jax.shard_map(on_device, mesh=mesh, in_specs=in_specs, out_specs=out_specs, check_vma=False)
```

```python
import functools

import jax
import jax.numpy as jnp
from jax import lax
from jax.experimental import pallas as pl
from jax.experimental.pallas import tpu as pltpu
from jax.sharding import Mesh
from jax.sharding import PartitionSpec as P

AXES = ("x", "zl", "core", "y", "zh")
SIZES = (4, 8, 2, 4, 2)
F32 = jnp.float32
BF16 = jnp.bfloat16


def index_of(x, zl, core, y, zh):
    return (((x * 8 + zl) * 2 + core) * 4 + y) * 2 + zh


def pairs(dest):
    out = []
    for x in range(4):
        for zl in range(8):
            for core in range(2):
                for y in range(4):
                    for zh in range(2):
                        out.append((index_of(x, zl, core, y, zh), index_of(*dest(x, zl, core, y, zh))))
    return out


def contract(a, b, da, db):
    return lax.dot_general(a, b, (((da,), (db,)), ((), ())), preferred_element_type=F32)


def prepare_kernel(first_ref, image_ref, system_ref, a_ref, fwd_ref, rinv_ref, col_ref):
    g = pl.program_id(0)
    low = lax.broadcasted_iota(jnp.int32, (64, 128), 1) < 64
    for p in range(16):
        f = first_ref[g, p]
        t0 = system_ref[0, p, 0].astype(F32)
        t1 = system_ref[0, p, 1].astype(F32)
        even = f % 2 == 0
        e = jnp.where(even, t0, t1)
        o = jnp.where(even, t1, t0)
        x0 = jnp.where(low, e, pltpu.roll(o, 64, 1))
        x1 = jnp.where(low, pltpu.roll(e, 64, 1), o)
        ve = jnp.where((f == 1) | (f == 2), 1, 0)
        vo = jnp.where(f >= 2, 1, 0)
        place = jnp.where(low, ve, vo)
        for t, xt in ((0, x0), (1, x1)):
            for v in range(2):
                a_ref[0, p * 64 : (p + 1) * 64, t * 256 + v * 128 : t * 256 + (v + 1) * 128] = jnp.where(
                    place == v, xt, 0.0
                ).astype(BF16)
    a = a_ref[0]
    fwd_ref[0] = contract(image_ref[...], a, 1, 0)
    rows = contract(jnp.ones((8, 1024), BF16), a, 1, 0)
    rinv_ref[0] = 1.0 / rows
    cols = contract(jnp.ones((8, 512), BF16), a, 1, 1)

    @pl.when(g == 0)
    def _():
        col_ref[...] = cols

    @pl.when(g > 0)
    def _():
        col_ref[...] += cols


def prepare(first, image, system):
    return pl.pallas_call(
        prepare_kernel,
        grid=(4,),
        in_specs=[
            pl.BlockSpec(memory_space=pltpu.SMEM),
            pl.BlockSpec((256, 1024), lambda g: (0, 0)),
            pl.BlockSpec((1, 16, 2, 64, 128), lambda g: (g, 0, 0, 0, 0)),
        ],
        out_specs=[
            pl.BlockSpec((1, 1024, 512), lambda g: (g, 0, 0)),
            pl.BlockSpec((1, 256, 512), lambda g: (g, 0, 0)),
            pl.BlockSpec((1, 8, 512), lambda g: (g, 0, 0)),
            pl.BlockSpec((8, 1024), lambda g: (0, 0)),
        ],
        out_shape=[
            jax.ShapeDtypeStruct((4, 1024, 512), BF16),
            jax.ShapeDtypeStruct((4, 256, 512), F32),
            jax.ShapeDtypeStruct((4, 8, 512), F32),
            jax.ShapeDtypeStruct((8, 1024), F32),
        ],
        cost_estimate=pl.CostEstimate(flops=1100000000, bytes_accessed=10000000, transcendentals=0),
        compiler_params=pltpu.CompilerParams(vmem_limit_bytes=24 * 1024 * 1024),
        name="prepare",
    )(first, image, system)


def pack_kernel(where_ref, p_ref, n0_ref, n1_ref, n2_ref, n3_ref, far_ref, sems):
    x, dl, zh = where_ref[0], where_ref[1], where_ref[2]
    copies = []
    for b, near_ref in enumerate((n0_ref, n1_ref, n2_ref, n3_ref)):
        low = dl ^ b
        copies.append(pltpu.make_async_copy(p_ref.at[:, (zh ^ (low & 1)) * 4 + low], near_ref, sems.at[b]))
    for m in range(4):
        for low in range(4):
            src = p_ref.at[x ^ m, (zh ^ (low & 1) ^ 1) * 4 + low]
            copies.append(pltpu.make_async_copy(src, far_ref.at[:, m, low], sems.at[4 + m * 4 + low]))
    for copy in copies:
        copy.start()
    for copy in copies:
        copy.wait()


def pack(where, projections):
    vmem = pl.BlockSpec(memory_space=pltpu.VMEM)
    return pl.pallas_call(
        pack_kernel,
        in_specs=[pl.BlockSpec(memory_space=pltpu.SMEM), pl.BlockSpec(memory_space=pl.ANY)],
        out_specs=[vmem] * 5,
        out_shape=[jax.ShapeDtypeStruct((4, 2, 32, 256), BF16)] * 4 + [jax.ShapeDtypeStruct((2, 4, 4, 32, 256), BF16)],
        scratch_shapes=[pltpu.SemaphoreType.DMA((20,))],
        cost_estimate=pl.CostEstimate(flops=0, bytes_accessed=2097152, transcendentals=0),
        compiler_params=pltpu.CompilerParams(vmem_limit_bytes=8 * 1024 * 1024),
        name="pack",
    )(where.astype(jnp.int32), projections.reshape(4, 8, 2, 32, 256))


def finish_kernel(where_ref, *refs):
    near_ref, far_refs, (a_ref, fwd_ref, rinv_ref, col_ref, res_ref, part_ref, held_ref) = refs[0], refs[1:5], refs[5:]
    dh, dl, own_y = where_ref[0], where_ref[1], where_ref[2]
    for b in range(4):
        g = dl ^ b
        for a in range(2):
            zh = dh ^ (dl & 1) ^ a
            for t in range(2):
                rinv = rinv_ref[g, 0:1, t * 256 : (t + 1) * 256]
                for y in range(4):
                    rows = pl.ds(pl.multiple_of((y * 2 + zh) * 32, 32), 32)
                    lanes = slice(t * 256, (t + 1) * 256)
                    block = near_ref[(y ^ own_y) * 2 + t, b] if a == 0 else far_refs[b][t * 4 + y]
                    res = ((block.astype(F32) - fwd_ref[g, rows, lanes]) * rinv).astype(BF16)
                    res_ref[g * 2 + t, rows, :] = res
                    held_ref[rows, lanes] = res
        for q in range(4):
            add = contract(held_ref[...], a_ref[g, q * 256 : (q + 1) * 256, :], 1, 1)
            if b == 0:
                part_ref[q, 0:256, :] = add
            else:
                part_ref[q, 0:256, :] += add
    row = lax.broadcasted_iota(jnp.int32, (16, 256), 0)
    for q in range(4):
        cols = col_ref[0:1, q * 256 : (q + 1) * 256]
        high = cols.astype(BF16).astype(F32)
        part_ref[q, 256:272, :] = jnp.where(row == 0, high, jnp.where(row == 1, cols - high, 0.0))


def finish(where, near, far, a, fwd, rinv, col):
    vmem = pl.BlockSpec(memory_space=pltpu.VMEM)
    return pl.pallas_call(
        finish_kernel,
        in_specs=[pl.BlockSpec(memory_space=pltpu.SMEM)] + [vmem] * 9,
        out_specs=[vmem, vmem],
        out_shape=[
            jax.ShapeDtypeStruct((8, 256, 256), BF16),
            jax.ShapeDtypeStruct((4, 272, 256), F32),
        ],
        scratch_shapes=[pltpu.VMEM((256, 512), BF16)],
        cost_estimate=pl.CostEstimate(flops=1100000000, bytes_accessed=10000000, transcendentals=0),
        compiler_params=pltpu.CompilerParams(vmem_limit_bytes=24 * 1024 * 1024),
        name="finish",
    )(where, near, *far, a, fwd, rinv, col)


def on_device(projections, start_image, system, first_tile):
    x, zl, y, zh = (lax.axis_index(name) for name in ("x", "zl", "y", "zh"))
    dh, dl = zl // 4, zl % 4
    def send(block, half, b):
        def dest(x, zl, core, y, zh):
            low = (zl % 4) ^ b
            return (x ^ y, (zh ^ (low & 1) ^ half) * 4 + low, core, x, zl // 4)

        return lax.ppermute(block, AXES, pairs(dest))

    *near, far = pack(jnp.stack([x, dl, zh]), projections)
    first_tile, image, system, far = lax.optimization_barrier((first_tile, start_image, system, far))
    near = [send(block.reshape(8, 32, 256), 0, b) for b, block in enumerate(near)]
    far = lax.all_to_all(far.reshape(8, 4, 32, 256), ("core", "y"), 0, 0, tiled=True)
    near, _ = lax.optimization_barrier((near, far))
    far = [lax.dynamic_index_in_dim(far, dl ^ b, 1, keepdims=False) for b in range(4)]
    near = jnp.stack(near, 1)
    far = [send(block, 1, b) for b, block in enumerate(far)]
    near = lax.all_to_all(near, ("x", "core"), 0, 0, tiled=True)
    a, fwd, rinv, col = prepare(first_tile, image, system)
    where = jnp.stack([dh, dl, y]).astype(jnp.int32)
    residual, part = finish(where, near, far, a, fwd, rinv, col)
    part = lax.all_to_all(part.astype(jnp.float16), "y", 0, 0, tiled=True).astype(F32).sum(0)
    halves = jnp.stack([part[:, :128], part[:, 128:]])
    mine = lax.dynamic_index_in_dim(halves, zh, 0, keepdims=False)
    other = lax.dynamic_index_in_dim(halves, 1 - zh, 0, keepdims=False)
    cols = other[256:257] + other[257:258]
    high = lax.reduce_precision(cols, 8, 7)
    other = jnp.concatenate([other[:256], high, cols - high, jnp.zeros((14, 128), F32)]).astype(jnp.float16)
    swap = pairs(lambda x, zl, core, y, zh: (x, zl, core, y, 1 - zh))
    total = mine + lax.ppermute(other, AXES, swap).astype(F32)
    local = lax.dynamic_slice_in_dim(start_image, (y * 2 + zh) * 128, 128, 1).astype(F32)
    new_image = local + total[:256] / (total[256:257] + total[257:258])
    return new_image, residual


def solution(mesh):
    mesh = Mesh(mesh.devices.reshape(SIZES), AXES)
    cuts, ang = ("x", "zl", "core"), ("y", "zh")
    in_specs = (
        P(cuts, None, ang, None, None),
        P(cuts, None),
        P(ang, None, None, None, None),
        P(ang, None),
    )
    out_specs = (P(cuts, ang), P(ang, cuts, None))
    return jax.shard_map(on_device, mesh=mesh, in_specs=in_specs, out_specs=out_specs, check_vma=False)
```

```python
import functools

import jax
import jax.numpy as jnp
from jax import lax
from jax.experimental import pallas as pl
from jax.experimental.pallas import tpu as pltpu
from jax.sharding import Mesh
from jax.sharding import PartitionSpec as P

AXES = ("x", "zl", "core", "y", "zh")
SIZES = (4, 8, 2, 4, 2)
NEAR = (0, 1, 2, 3)
FAR = (5, 4, 7, 6)
F32 = jnp.float32
BF16 = jnp.bfloat16


def index_of(x, zl, core, y, zh):
    return (((x * 8 + zl) * 2 + core) * 4 + y) * 2 + zh


def mixed(place):
    return place ^ ((place & 1) * 4)


def pairs(dest):
    out = []
    for x in range(4):
        for zl in range(8):
            for core in range(2):
                for y in range(4):
                    for zh in range(2):
                        out.append((index_of(x, zl, core, y, zh), index_of(*dest(x, zl, core, y, zh))))
    return out


def contract(a, b, da, db):
    return lax.dot_general(a, b, (((da,), (db,)), ((), ())), preferred_element_type=F32)


def prepare_kernel(first_ref, image_ref, system_ref, a_ref, fwd_ref, rinv_ref, col_ref):
    g = pl.program_id(0)
    low = lax.broadcasted_iota(jnp.int32, (64, 128), 1) < 64
    for p in range(16):
        f = first_ref[g, p]
        t0 = system_ref[0, p, 0].astype(F32)
        t1 = system_ref[0, p, 1].astype(F32)
        even = f % 2 == 0
        e = jnp.where(even, t0, t1)
        o = jnp.where(even, t1, t0)
        x0 = jnp.where(low, e, pltpu.roll(o, 64, 1))
        x1 = jnp.where(low, pltpu.roll(e, 64, 1), o)
        ve = jnp.where((f == 1) | (f == 2), 1, 0)
        vo = jnp.where(f >= 2, 1, 0)
        place = jnp.where(low, ve, vo)
        for t, xt in ((0, x0), (1, x1)):
            for v in range(2):
                a_ref[0, p * 64 : (p + 1) * 64, t * 256 + v * 128 : t * 256 + (v + 1) * 128] = jnp.where(
                    place == v, xt, 0.0
                ).astype(BF16)
    a = a_ref[0]
    fwd_ref[0] = contract(image_ref[...], a, 1, 0)
    rows = contract(jnp.ones((8, 1024), BF16), a, 1, 0)
    rinv_ref[0] = 1.0 / rows
    cols = contract(jnp.ones((8, 512), BF16), a, 1, 1)

    @pl.when(g == 0)
    def _():
        col_ref[...] = cols

    @pl.when(g > 0)
    def _():
        col_ref[...] += cols


def prepare(first, image, system):
    return pl.pallas_call(
        prepare_kernel,
        grid=(4,),
        in_specs=[
            pl.BlockSpec(memory_space=pltpu.SMEM),
            pl.BlockSpec((256, 1024), lambda g: (0, 0)),
            pl.BlockSpec((1, 16, 2, 64, 128), lambda g: (g, 0, 0, 0, 0)),
        ],
        out_specs=[
            pl.BlockSpec((1, 1024, 512), lambda g: (g, 0, 0)),
            pl.BlockSpec((1, 256, 512), lambda g: (g, 0, 0)),
            pl.BlockSpec((1, 8, 512), lambda g: (g, 0, 0)),
            pl.BlockSpec((8, 1024), lambda g: (0, 0)),
        ],
        out_shape=[
            jax.ShapeDtypeStruct((4, 1024, 512), BF16),
            jax.ShapeDtypeStruct((4, 256, 512), F32),
            jax.ShapeDtypeStruct((4, 8, 512), F32),
            jax.ShapeDtypeStruct((8, 1024), F32),
        ],
        cost_estimate=pl.CostEstimate(flops=1100000000, bytes_accessed=10000000, transcendentals=0),
        compiler_params=pltpu.CompilerParams(vmem_limit_bytes=24 * 1024 * 1024),
        name="prepare",
    )(first, image, system)


def pack_kernel(p_ref, *refs):
    far_ref, sems = refs[-2:]
    x, place = lax.axis_index("x"), lax.axis_index("zh") * 4 + lax.rem(lax.axis_index("zl"), 4)
    copies = []
    for n, k in enumerate(NEAR):
        copies.append(pltpu.make_async_copy(p_ref.at[:, mixed(place ^ k)], refs[n], sems.at[n]))
    for n, k in enumerate(FAR):
        for m in range(4):
            sem = sems.at[len(NEAR) + n * 4 + m]
            copies.append(pltpu.make_async_copy(p_ref.at[x ^ m, mixed(place ^ k)], far_ref.at[:, m, n], sem))
    for copy in copies:
        copy.start()
    for copy in copies:
        copy.wait()


def pack(projections):
    vmem = pl.BlockSpec(memory_space=pltpu.VMEM)
    return pl.pallas_call(
        pack_kernel,
        in_specs=[pl.BlockSpec(memory_space=pl.ANY)],
        out_specs=[vmem] * (len(NEAR) + 1),
        out_shape=[jax.ShapeDtypeStruct((4, 2, 32, 256), BF16)] * len(NEAR)
        + [jax.ShapeDtypeStruct((2, 4, len(FAR), 32, 256), BF16)],
        scratch_shapes=[pltpu.SemaphoreType.DMA((len(NEAR) + 4 * len(FAR),))],
        cost_estimate=pl.CostEstimate(flops=0, bytes_accessed=2097152, transcendentals=0),
        compiler_params=pltpu.CompilerParams(vmem_limit_bytes=60 * 1024 * 1024),
        name="pack",
    )(projections.reshape(4, 8, 2, 32, 256))


def finish_kernel(where_ref, *refs):
    near_ref, far_refs = refs[0], refs[1 : 1 + len(FAR)]
    a_ref, fwd_ref, rinv_ref, col_ref, res_ref, part_ref, held_ref = refs[1 + len(FAR) :]
    dh, dl, own_y = where_ref[0], where_ref[1], where_ref[2]
    for b in range(4):
        g = dl ^ b
        for a in range(2):
            zh = dh ^ (dl & 1) ^ a
            k = a * 4 + b
            for t in range(2):
                rinv = rinv_ref[g, 0:1, t * 256 : (t + 1) * 256]
                for y in range(4):
                    rows = pl.ds(pl.multiple_of((y * 2 + zh) * 32, 32), 32)
                    lanes = slice(t * 256, (t + 1) * 256)
                    if k in NEAR:
                        block = near_ref[(y ^ own_y) * 2 + t, NEAR.index(k)]
                    else:
                        block = far_refs[FAR.index(k)][t * 4 + y]
                    res = ((block.astype(F32) - fwd_ref[g, rows, lanes]) * rinv).astype(BF16)
                    res_ref[g * 2 + t, rows, :] = res
                    held_ref[rows, lanes] = res
        for q in range(4):
            add = contract(held_ref[...], a_ref[g, q * 256 : (q + 1) * 256, :], 1, 1)
            if b == 0:
                part_ref[q, 0:256, :] = add
            else:
                part_ref[q, 0:256, :] += add
    row = lax.broadcasted_iota(jnp.int32, (16, 256), 0)
    for q in range(4):
        cols = col_ref[0:1, q * 256 : (q + 1) * 256]
        high = cols.astype(BF16).astype(F32)
        part_ref[q, 256:272, :] = jnp.where(row == 0, high, jnp.where(row == 1, cols - high, 0.0))


def finish(where, near, far, a, fwd, rinv, col):
    vmem = pl.BlockSpec(memory_space=pltpu.VMEM)
    return pl.pallas_call(
        finish_kernel,
        in_specs=[pl.BlockSpec(memory_space=pltpu.SMEM)] + [vmem] * (5 + len(FAR)),
        out_specs=[vmem, vmem],
        out_shape=[
            jax.ShapeDtypeStruct((8, 256, 256), BF16),
            jax.ShapeDtypeStruct((4, 272, 256), F32),
        ],
        scratch_shapes=[pltpu.VMEM((256, 512), BF16)],
        cost_estimate=pl.CostEstimate(flops=1100000000, bytes_accessed=10000000, transcendentals=0),
        compiler_params=pltpu.CompilerParams(vmem_limit_bytes=24 * 1024 * 1024),
        name="finish",
    )(where, near, *far, a, fwd, rinv, col)


def on_device(projections, start_image, system, first_tile):
    zl, y, zh = (lax.axis_index(name) for name in ("zl", "y", "zh"))
    dh, dl = zl // 4, zl % 4
    def send(block, k):
        def dest(x, zl, core, y, zh):
            return (x ^ y, mixed((zh * 4 + zl % 4) ^ k), core, x, zl // 4)

        return lax.ppermute(block, AXES, pairs(dest))

    *near, far = pack(projections)
    near = [send(block.reshape(8, 32, 256), k) for k, block in zip(NEAR, near)]
    far = lax.all_to_all(far.reshape(8, len(FAR), 32, 256), ("core", "y"), 0, 0, tiled=True)
    near, _ = lax.optimization_barrier((near, far))
    near = jnp.stack(near, 1)
    far = [send(far[:, n], k) for n, k in enumerate(FAR)]
    near = lax.all_to_all(near, ("x", "core"), 0, 0, tiled=True)
    first_tile, image, system, near = lax.optimization_barrier((first_tile, start_image, system, near))
    local = lax.dynamic_slice_in_dim(image, (y * 2 + zh) * 128, 128, 1).astype(F32)
    a, fwd, rinv, col = prepare(first_tile, image, system)
    col, local = lax.optimization_barrier((col, local))
    where = jnp.stack([dh, dl, y]).astype(jnp.int32)
    residual, part = finish(where, near, far, a, fwd, rinv, col)
    part = lax.all_to_all(part.astype(jnp.float16), "y", 0, 0, tiled=True).astype(F32).sum(0)
    halves = jnp.stack([part[:, :128], part[:, 128:]])
    mine = lax.dynamic_index_in_dim(halves, zh, 0, keepdims=False)
    other = lax.dynamic_index_in_dim(halves, 1 - zh, 0, keepdims=False)
    cols = other[256:257] + other[257:258]
    high = lax.reduce_precision(cols, 8, 7)
    other = jnp.concatenate([other[:256], high, cols - high, jnp.zeros((14, 128), F32)]).astype(jnp.float16)
    swap = pairs(lambda x, zl, core, y, zh: (x, zl, core, y, 1 - zh))
    total = mine + lax.ppermute(other, AXES, swap).astype(F32)
    new_image = local + total[:256] / (total[256:257] + total[257:258])
    return new_image, residual


def solution(mesh):
    mesh = Mesh(mesh.devices.reshape(SIZES), AXES)
    cuts, ang = ("x", "zl", "core"), ("y", "zh")
    in_specs = (
        P(cuts, None, ang, None, None),
        P(cuts, None),
        P(ang, None, None, None, None),
        P(ang, None),
    )
    out_specs = (P(cuts, ang), P(ang, cuts, None))
    return jax.shard_map(on_device, mesh=mesh, in_specs=in_specs, out_specs=out_specs, check_vma=False)
```

```python
import functools

import jax
import jax.numpy as jnp
from jax import lax
from jax.experimental import pallas as pl
from jax.experimental.pallas import tpu as pltpu
from jax.sharding import Mesh
from jax.sharding import PartitionSpec as P

AXES = ("x", "zl", "core", "y", "zh")
SIZES = (4, 8, 2, 4, 2)
NEAR = (4, 5, 6, 7)
FAR = (0, 1, 2, 3)
F32 = jnp.float32
BF16 = jnp.bfloat16


def index_of(x, zl, core, y, zh):
    return (((x * 8 + zl) * 2 + core) * 4 + y) * 2 + zh


def mixed(place):
    return place ^ ((place & 1) * 4)


def pairs(dest):
    out = []
    for x in range(4):
        for zl in range(8):
            for core in range(2):
                for y in range(4):
                    for zh in range(2):
                        out.append((index_of(x, zl, core, y, zh), index_of(*dest(x, zl, core, y, zh))))
    return out


def contract(a, b, da, db):
    return lax.dot_general(a, b, (((da,), (db,)), ((), ())), preferred_element_type=F32)


def prepare_kernel(first_ref, image_ref, system_ref, a_ref, fwd_ref, rinv_ref, col_ref):
    g = pl.program_id(0)
    low = lax.broadcasted_iota(jnp.int32, (64, 128), 1) < 64
    for p in range(16):
        f = first_ref[g, p]
        t0 = system_ref[0, p, 0].astype(F32)
        t1 = system_ref[0, p, 1].astype(F32)
        even = f % 2 == 0
        e = jnp.where(even, t0, t1)
        o = jnp.where(even, t1, t0)
        x0 = jnp.where(low, e, pltpu.roll(o, 64, 1))
        x1 = jnp.where(low, pltpu.roll(e, 64, 1), o)
        ve = jnp.where((f == 1) | (f == 2), 1, 0)
        vo = jnp.where(f >= 2, 1, 0)
        place = jnp.where(low, ve, vo)
        for t, xt in ((0, x0), (1, x1)):
            for v in range(2):
                a_ref[0, p * 64 : (p + 1) * 64, t * 256 + v * 128 : t * 256 + (v + 1) * 128] = jnp.where(
                    place == v, xt, 0.0
                ).astype(BF16)
    a = a_ref[0]
    fwd_ref[0] = contract(image_ref[...], a, 1, 0)
    rows = contract(jnp.ones((8, 1024), BF16), a, 1, 0)
    rinv_ref[0] = 1.0 / rows
    cols = contract(jnp.ones((8, 512), BF16), a, 1, 1)

    @pl.when(g == 0)
    def _():
        col_ref[...] = cols

    @pl.when(g > 0)
    def _():
        col_ref[...] += cols


def prepare(first, image, system):
    return pl.pallas_call(
        prepare_kernel,
        grid=(4,),
        in_specs=[
            pl.BlockSpec(memory_space=pltpu.SMEM),
            pl.BlockSpec((256, 1024), lambda g: (0, 0)),
            pl.BlockSpec((1, 16, 2, 64, 128), lambda g: (g, 0, 0, 0, 0)),
        ],
        out_specs=[
            pl.BlockSpec((1, 1024, 512), lambda g: (g, 0, 0)),
            pl.BlockSpec((1, 256, 512), lambda g: (g, 0, 0)),
            pl.BlockSpec((1, 8, 512), lambda g: (g, 0, 0)),
            pl.BlockSpec((8, 1024), lambda g: (0, 0)),
        ],
        out_shape=[
            jax.ShapeDtypeStruct((4, 1024, 512), BF16),
            jax.ShapeDtypeStruct((4, 256, 512), F32),
            jax.ShapeDtypeStruct((4, 8, 512), F32),
            jax.ShapeDtypeStruct((8, 1024), F32),
        ],
        cost_estimate=pl.CostEstimate(flops=1100000000, bytes_accessed=10000000, transcendentals=0),
        compiler_params=pltpu.CompilerParams(vmem_limit_bytes=24 * 1024 * 1024),
        name="prepare",
    )(first, image, system)


def pack_kernel(p_ref, *refs):
    far_ref, sems = refs[-2:]
    x, place = lax.axis_index("x"), lax.axis_index("zh") * 4 + lax.rem(lax.axis_index("zl"), 4)
    copies = []
    for n, k in enumerate(NEAR):
        copies.append(pltpu.make_async_copy(p_ref.at[:, mixed(place ^ k)], refs[n], sems.at[n]))
    for n, k in enumerate(FAR):
        for m in range(4):
            sem = sems.at[len(NEAR) + n * 4 + m]
            copies.append(pltpu.make_async_copy(p_ref.at[x ^ m, mixed(place ^ k)], far_ref.at[:, m, n], sem))
    for copy in copies:
        copy.start()
    for copy in copies:
        copy.wait()


def pack(projections):
    vmem = pl.BlockSpec(memory_space=pltpu.VMEM)
    return pl.pallas_call(
        pack_kernel,
        in_specs=[pl.BlockSpec(memory_space=pl.ANY)],
        out_specs=[vmem] * (len(NEAR) + 1),
        out_shape=[jax.ShapeDtypeStruct((4, 2, 32, 256), BF16)] * len(NEAR)
        + [jax.ShapeDtypeStruct((2, 4, len(FAR), 32, 256), BF16)],
        scratch_shapes=[pltpu.SemaphoreType.DMA((len(NEAR) + 4 * len(FAR),))],
        cost_estimate=pl.CostEstimate(flops=0, bytes_accessed=2097152, transcendentals=0),
        compiler_params=pltpu.CompilerParams(vmem_limit_bytes=60 * 1024 * 1024),
        name="pack",
    )(projections.reshape(4, 8, 2, 32, 256))


def finish_kernel(where_ref, *refs):
    near_ref, far_refs = refs[0], refs[1 : 1 + len(FAR)]
    a_ref, fwd_ref, rinv_ref, col_ref, res_ref, part_ref, held_ref = refs[1 + len(FAR) :]
    dh, dl, own_y = where_ref[0], where_ref[1], where_ref[2]
    for b in range(4):
        g = dl ^ b
        for a in range(2):
            zh = dh ^ (dl & 1) ^ a
            k = a * 4 + b
            for t in range(2):
                rinv = rinv_ref[g, 0:1, t * 256 : (t + 1) * 256]
                for y in range(4):
                    rows = pl.ds(pl.multiple_of((y * 2 + zh) * 32, 32), 32)
                    lanes = slice(t * 256, (t + 1) * 256)
                    if k in NEAR:
                        block = near_ref[(y ^ own_y) * 2 + t, NEAR.index(k)]
                    else:
                        block = far_refs[FAR.index(k)][t * 4 + y]
                    res = ((block.astype(F32) - fwd_ref[g, rows, lanes]) * rinv).astype(BF16)
                    res_ref[g * 2 + t, rows, :] = res
                    held_ref[rows, lanes] = res
        for q in range(4):
            add = contract(held_ref[...], a_ref[g, q * 256 : (q + 1) * 256, :], 1, 1)
            if b == 0:
                part_ref[q, 0:256, :] = add
            else:
                part_ref[q, 0:256, :] += add
    row = lax.broadcasted_iota(jnp.int32, (16, 256), 0)
    for q in range(4):
        cols = col_ref[0:1, q * 256 : (q + 1) * 256]
        high = cols.astype(BF16).astype(F32)
        part_ref[q, 256:272, :] = jnp.where(row == 0, high, jnp.where(row == 1, cols - high, 0.0))


def finish(where, near, far, a, fwd, rinv, col):
    vmem = pl.BlockSpec(memory_space=pltpu.VMEM)
    return pl.pallas_call(
        finish_kernel,
        in_specs=[pl.BlockSpec(memory_space=pltpu.SMEM)] + [vmem] * (5 + len(FAR)),
        out_specs=[vmem, vmem],
        out_shape=[
            jax.ShapeDtypeStruct((8, 256, 256), BF16),
            jax.ShapeDtypeStruct((4, 272, 256), F32),
        ],
        scratch_shapes=[pltpu.VMEM((256, 512), BF16)],
        cost_estimate=pl.CostEstimate(flops=1100000000, bytes_accessed=10000000, transcendentals=0),
        compiler_params=pltpu.CompilerParams(vmem_limit_bytes=24 * 1024 * 1024),
        name="finish",
    )(where, near, *far, a, fwd, rinv, col)


def on_device(projections, start_image, system, first_tile):
    zl, y, zh = (lax.axis_index(name) for name in ("zl", "y", "zh"))
    dh, dl = zl // 4, zl % 4
    def send(block, k):
        def dest(x, zl, core, y, zh):
            return (x ^ y, mixed((zh * 4 + zl % 4) ^ k), core, x, zl // 4)

        return lax.ppermute(block, AXES, pairs(dest))

    *near, far = pack(projections)
    near = [send(block.reshape(8, 32, 256), k) for k, block in zip(NEAR, near)]
    far = lax.all_to_all(far.reshape(8, len(FAR), 32, 256), ("core", "y"), 0, 0, tiled=True)
    near, _ = lax.optimization_barrier((near, far))
    near = jnp.stack(near, 1)
    far = [send(far[:, n], k) for n, k in enumerate(FAR)]
    near = lax.all_to_all(near, ("x", "core"), 0, 0, tiled=True)
    first_tile, image, system, near = lax.optimization_barrier((first_tile, start_image, system, near))
    local = lax.dynamic_slice_in_dim(image, (y * 2 + zh) * 128, 128, 1).astype(F32)
    a, fwd, rinv, col = prepare(first_tile, image, system)
    col, local = lax.optimization_barrier((col, local))
    where = jnp.stack([dh, dl, y]).astype(jnp.int32)
    residual, part = finish(where, near, far, a, fwd, rinv, col)
    part = lax.all_to_all(part.astype(jnp.float16), "y", 0, 0, tiled=True).astype(F32).sum(0)
    halves = jnp.stack([part[:, :128], part[:, 128:]])
    mine = lax.dynamic_index_in_dim(halves, zh, 0, keepdims=False)
    other = lax.dynamic_index_in_dim(halves, 1 - zh, 0, keepdims=False)
    cols = other[256:257] + other[257:258]
    high = lax.reduce_precision(cols, 8, 7)
    other = jnp.concatenate([other[:256], high, cols - high, jnp.zeros((14, 128), F32)]).astype(jnp.float16)
    swap = pairs(lambda x, zl, core, y, zh: (x, zl, core, y, 1 - zh))
    total = mine + lax.ppermute(other, AXES, swap).astype(F32)
    new_image = local + total[:256] / (total[256:257] + total[257:258])
    return new_image, residual


def solution(mesh):
    mesh = Mesh(mesh.devices.reshape(SIZES), AXES)
    cuts, ang = ("x", "zl", "core"), ("y", "zh")
    in_specs = (
        P(cuts, None, ang, None, None),
        P(cuts, None),
        P(ang, None, None, None, None),
        P(ang, None),
    )
    out_specs = (P(cuts, ang), P(ang, cuts, None))
    return jax.shard_map(on_device, mesh=mesh, in_specs=in_specs, out_specs=out_specs, check_vma=False)
```
